128 devices in a mesh: section: 16 (over x, y), tp: 8 (over z, core).
Axes of the slice: x: 4, y: 4, z: 4, core: 2. Of those that a mesh axis runs over, the one named last changes fastest.
Arguments:
- queries: bfloat16 [4096, 4096], P(('section', 'tp')), may hold values from -256 to 256
- keys: bfloat16 [4096, 4096], P(('section', 'tp')), may hold values from -8 to 8
- values: bfloat16 [4096, 4096], P(('section', 'tp')), may hold values from -72 to 72
- out_grad: bfloat16 [4096, 4096], P(('section', 'tp')), may hold values from -6 to 6
- lam: float32 [16], P('tp'), may hold values from 0.2 to 0.9
- lengths: int32 [16], replicated, may hold values from 128 to 256, as said below
Outputs:
- query_grad: bfloat16 [4096, 4096], P(('section', 'tp'))
- key_grad: bfloat16 [4096, 4096], P(('section', 'tp'))
- value_grad: bfloat16 [4096, 4096], P(('section', 'tp'))
The draws below stay inside these ranges and needn't reach their ends.
Inputs may be any that keep to these rules, and one draw needn't show every extreme that they name: `lengths`: each slice holds 128 to 256 live tokens, never more in a later slice than in an earlier one; the first slice is full.
All inputs are finite; a program needn't handle non-finite values.
Results may differ from the reference program's by a relative error of at most 0.017.
Values may be sent and summed in bfloat16 or wider, within the bound.
No kernel may reach another device: no remote copies, remote signals or barrier semaphores. Data moves between devices by JAX's collectives and lax.ppermute only.
A program may use at most 128 MiB of HBM per device.

```python
import math
import jax
import jax.numpy as jnp
from jax import lax

H = 16
DH = 128
CAP = 256
NSLICE = 16
TOTAL = 4096
D = 4096
N_SECTION = 16


def paired_fields(key, weight):
    key_base, key_query = jax.random.split(key, 2)
    pos = jnp.arange(TOTAL, dtype=jnp.int32)[:, None]
    base = jnp.clip(jax.random.normal(key_base, (TOTAL, D), jnp.float32), -6.0, 6.0)
    after = (pos % CAP == CAP // 4 - CAP // 8).astype(jnp.float32) * weight
    key_field = base * (1.0 - after)
    query_base = jnp.clip(jax.random.normal(key_query, (TOTAL, D), jnp.float32), -6.0, 6.0)
    chosen = (pos % CAP == CAP // 4).astype(jnp.float32) * weight
    query_field = query_base * (1.0 - chosen)
    return (query_field, key_field)


def draw_queries(key, part):
    query_field, key_field = paired_fields(key, 0.0)
    return query_field.astype(jnp.bfloat16)


def draw_keys(key, part):
    query_field, key_field = paired_fields(key, 0.0)
    return key_field.astype(jnp.bfloat16)


def draw_values(key, part):
    key = jax.random.fold_in(key, 7)
    key_base, key_rows, key_cols = jax.random.split(key, 3)
    base = jnp.clip(jax.random.normal(key_base, (TOTAL, D), jnp.float32), -6.0, 6.0)
    row_scale = jnp.exp(jax.random.uniform(key_rows, (TOTAL, 1), jnp.float32, -1.2, 1.2))
    col_scale = jnp.exp(jax.random.uniform(key_cols, (1, D), jnp.float32, -1.2, 1.2))
    return (base * row_scale * col_scale).astype(jnp.bfloat16)


def draw_lengths(key, part):
    key = jax.random.fold_in(key, 11)
    counts = jax.random.randint(key, (NSLICE,), CAP // 2, CAP + 1, jnp.int32)
    counts = -jnp.sort(-counts)
    return counts.at[0].set(CAP)


def block_scale(own_key, shape, cuts, smallest, largest):
    gain, own = 1.0, jax.random.fold_in(own_key, 6)
    for dim, shards_of in cuts:
        heights = jnp.exp(jax.random.uniform(jax.random.fold_in(own, dim), (shards_of,), jnp.float32, smallest / len(cuts), largest / len(cuts)))
        gain = gain * jnp.repeat(heights, shape[dim] // shards_of).reshape([-1 if axis == dim else 1 for axis in range(len(shape))])
    return gain


def centred(key, shape, scale, bound, cuts=(), kind=jnp.bfloat16):
    loudness = block_scale(key, shape, cuts, -0.22, 0.18) if cuts else 1.0
    entries = jax.random.normal(key, shape, jnp.float32) * scale * loudness
    return jnp.minimum(jnp.maximum(entries, -bound), bound).astype(kind)


def setup_inputs(seed: int = 0) -> dict:
    arg_keys = jax.random.split(jax.random.key(seed), 7)
    queries = draw_queries(jax.random.fold_in(arg_keys[6], 71), 0)
    keys = draw_keys(jax.random.fold_in(arg_keys[6], 71), 0)
    values = draw_values(jax.random.fold_in(arg_keys[6], 71), 0)
    out_grad = centred(arg_keys[3], (TOTAL, D), 1.0, 6.0, ((0, 128),))
    lam = jnp.clip(jnp.exp(math.log(0.9) - 1.50407736 * jax.random.uniform(arg_keys[4], (H,), jnp.float32) ** block_scale(arg_keys[4], (H,), ((0, 8),), -0.2, 0.2)), 0.2, 0.9)
    lengths = draw_lengths(jax.random.fold_in(arg_keys[6], 71), 0)
    return dict(queries=queries, keys=keys, values=values, out_grad=out_grad, lam=lam, lengths=lengths)


EPSILON = 1e-05
NEGATIVE = -1e+30

def masked_scores(qpart, kpart, visible, scale):
    scores = jnp.dot(qpart, kpart.T, preferred_element_type=jnp.float32) * scale
    return jnp.where(visible, scores, NEGATIVE)

def softmax_parts(scores):
    top = lax.optimization_barrier(jnp.max(scores, axis=1, keepdims=True))
    total = lax.optimization_barrier(jnp.sum(jnp.exp(scores - top), axis=1, keepdims=True))
    return (top, total)

def head_forward(qh, kh, vh, gh, weight, visible, scale, half):
    s_one = masked_scores(qh[:, :half], kh[:, :half], visible, scale)
    s_two = masked_scores(qh[:, half:], kh[:, half:], visible, scale)
    m_one, l_one = softmax_parts(s_one)
    m_two, l_two = softmax_parts(s_two)
    p_one = jnp.exp(s_one - m_one) / l_one
    p_two = jnp.exp(s_two - m_two) / l_two
    mixed = (p_one - weight * p_two).astype(jnp.bfloat16)
    output = jnp.dot(mixed, vh, preferred_element_type=jnp.float32)
    factor = lax.rsqrt(lax.optimization_barrier(jnp.mean(output * output, axis=1, keepdims=True)) + EPSILON)
    normed = output * factor
    d_out = (factor * (gh - normed * lax.optimization_barrier(jnp.mean(gh * normed, axis=1, keepdims=True)))).astype(jnp.bfloat16)
    d_mix = jnp.dot(d_out, vh.T, preferred_element_type=jnp.float32)
    e_one = lax.optimization_barrier(jnp.sum(d_mix * p_one, axis=1, keepdims=True))
    e_two = lax.optimization_barrier(jnp.sum(d_mix * p_two, axis=1, keepdims=True))
    t_one = (scale * p_one * (d_mix - e_one)).astype(jnp.bfloat16)
    t_two = (-scale * weight * p_two * (d_mix - e_two)).astype(jnp.bfloat16)
    d_query = jnp.concatenate([jnp.dot(t_one, kh[:, :half], preferred_element_type=jnp.float32), jnp.dot(t_two, kh[:, half:], preferred_element_type=jnp.float32)], axis=1)
    return (d_query, mixed, d_out, t_one, t_two)

def section_sum(left, right):
    total = left.shape[1]
    parts = jnp.einsum('nck,ncd->nkd', left.reshape(N_SECTION, CAP, total).astype(jnp.float32), right.reshape(N_SECTION, CAP, right.shape[1]).astype(jnp.float32))
    rounded = lax.optimization_barrier(parts.astype(jnp.bfloat16))
    return lax.optimization_barrier(jnp.sum(rounded.astype(jnp.float32), axis=0)).astype(jnp.bfloat16)

def reference(queries, keys, values, out_grad, lam, lengths):
    total = CAP * N_SECTION
    width = 2 * DH
    scale = DH ** (-0.5)
    pos = jnp.arange(total, dtype=jnp.int32)
    valid = pos % CAP < lengths[pos // CAP]
    visible = (pos[None, :] <= pos[:, None]) & valid[None, :]
    qmask = valid.astype(jnp.float32)[:, None]

    def heads_first(x):
        return x.reshape(total, H, width).transpose(1, 0, 2)

    def one_head(items):
        qh, kh, vh, gh, weight = items
        d_query, mixed, d_out, t_one, t_two = head_forward(qh, kh, vh, gh.astype(jnp.float32) * qmask, weight, visible, scale, DH)
        d_key = jnp.concatenate([section_sum(t_one, qh[:, :DH]), section_sum(t_two, qh[:, DH:])], axis=1)
        d_value = section_sum(mixed, d_out)
        return (d_query.astype(jnp.bfloat16), d_key, d_value)
    d_query, d_key, d_value = lax.map(one_head, (heads_first(queries), heads_first(keys), heads_first(values), heads_first(out_grad), lam))

    def rows_first(x):
        return x.transpose(1, 0, 2).reshape(total, H * width)
    return (rows_first(d_query), rows_first(d_key), rows_first(d_value))
```

```python
import functools

import jax
import jax.numpy as jnp
from jax import lax
from jax.experimental import pallas as pl
from jax.experimental.pallas import tpu as pltpu
from jax.sharding import Mesh
from jax.sharding import PartitionSpec as P

EPSILON = 1e-05
NEGATIVE = -1e30
LOG2E = 1.4426950408889634

STRIPE = 32
SLICES = 16
PARTS = 8
WIDTH = 256
HALF = 128
TILE = 128
GROUPS = 4
CHUNK = PARTS * TILE
ROWS = GROUPS * TILE
SECTION = ("x", "y")
SCALE = HALF ** (-0.5)


def pack_kernel(a_ref, b_ref, out_ref):
    for head in range(SLICES):
        cols = slice(head * WIDTH, (head + 1) * WIDTH)
        out_ref[head, 0] = a_ref[:, cols]
        out_ref[head, 1] = b_ref[:, cols]


def pack(a, b):
    return pl.pallas_call(
        pack_kernel,
        out_shape=jax.ShapeDtypeStruct((SLICES, 2, STRIPE, WIDTH), a.dtype),
        in_specs=[pl.BlockSpec(memory_space=pltpu.VMEM)] * 2,
        out_specs=pl.BlockSpec(memory_space=pltpu.VMEM),
        name="pack",
    )(a, b)


def unpack_pair_kernel(in_ref, a_ref, b_ref):
    for head in range(SLICES):
        cols = slice(head * WIDTH, (head + 1) * WIDTH)
        a_ref[:, cols] = in_ref[head, 0]
        b_ref[:, cols] = in_ref[head, 1]


def unpack_pair(x):
    shape = jax.ShapeDtypeStruct((STRIPE, SLICES * WIDTH), x.dtype)
    return pl.pallas_call(
        unpack_pair_kernel,
        out_shape=(shape, shape),
        in_specs=[pl.BlockSpec(memory_space=pltpu.VMEM)],
        out_specs=(pl.BlockSpec(memory_space=pltpu.VMEM),) * 2,
        name="unpack_pair",
    )(x)


def unpack_one_kernel(in_ref, a_ref):
    for head in range(SLICES):
        a_ref[:, head * WIDTH : (head + 1) * WIDTH] = in_ref[head]


def unpack_one(x):
    return pl.pallas_call(
        unpack_one_kernel,
        out_shape=jax.ShapeDtypeStruct((STRIPE, SLICES * WIDTH), x.dtype),
        in_specs=[pl.BlockSpec(memory_space=pltpu.VMEM)],
        out_specs=pl.BlockSpec(memory_space=pltpu.VMEM),
        name="unpack_one",
    )(x)


def dot_nt(a, b):
    return lax.dot_general(a, b, (((1,), (1,)), ((), ())), preferred_element_type=jnp.float32)


def dot_nn(a, b):
    return lax.dot_general(a, b, (((1,), (0,)), ((), ())), preferred_element_type=jnp.float32)


def dot_tn(a, b):
    return lax.dot_general(a, b, (((0,), (0,)), ((), ())), preferred_element_type=jnp.float32)


def fold(op, x):
    out = x[:, :128]
    for c in range(1, CHUNK // 128):
        out = op(out, x[:, c * 128 : (c + 1) * 128])
    return out


def core_kernel(lengths, where, lam, qg, *refs):
    kv_parts = refs[:PARTS]
    dq_out, own_out, sib_out = refs[PARTS : PARTS + 3]
    ks, vs, p1s, p2s, das, mixs, t1s, t2s, key_pos, sems = refs[PARTS + 3 :]

    copies = []
    for u in range(PARTS):
        for kind, dst in ((0, ks), (1, vs)):
            for j in range(GROUPS):
                copy = pltpu.make_async_copy(
                    kv_parts[u].at[pl.ds(4 * j, 4), kind],
                    dst.at[j, u],
                    sems.at[(u * 2 + kind) * GROUPS + j],
                )
                copy.start()
                copies.append(copy)

    lane = lax.broadcasted_iota(jnp.int32, (1, TILE), 1)
    for j in range(GROUPS):
        length = jnp.full((1, TILE), lengths[4 * j], jnp.int32)
        for nl in range(1, 4):
            length = jnp.where(lane // STRIPE == nl, lengths[4 * j + nl], length)
        for u in range(PARTS):
            slot = where[u] * STRIPE + lane % STRIPE
            pos = 256 * (4 * j + lane // STRIPE) + slot
            key_pos[j, :, u * TILE : (u + 1) * TILE] = jnp.where(slot < length, pos, 1 << 30)

    for copy in copies:
        copy.wait()

    weight = lam[0]
    row = lax.broadcasted_iota(jnp.int32, (TILE, 1), 0)
    row_pos = 256 * (row // STRIPE) + where[0] * STRIPE + row % STRIPE
    row_slot = where[0] * STRIPE + row % STRIPE
    zero128 = jnp.zeros((TILE, 128), jnp.float32)

    def tile(i, _):
        rows = pl.ds(pl.multiple_of(i * TILE, TILE), TILE)
        q = qg[pl.ds(i * 4, 4), 0].reshape(TILE, WIDTH)
        q1, q2 = q[:, :HALF], q[:, HALF:]
        qpos = row_pos + 1024 * i

        def scores(j, carry):
            m1, m2 = carry
            k = ks[j].reshape(CHUNK, WIDTH)
            vis = key_pos[j] <= qpos
            s1 = jnp.where(vis, dot_nt(q1, k[:, :HALF]), NEGATIVE)
            s2 = jnp.where(vis, dot_nt(q2, k[:, HALF:]), NEGATIVE)
            p1s[j] = s1
            p2s[j] = s2
            return jnp.maximum(m1, fold(jnp.maximum, s1)), jnp.maximum(m2, fold(jnp.maximum, s2))

        lowest = jnp.full((TILE, 128), NEGATIVE, jnp.float32)
        m1, m2 = lax.fori_loop(0, i + 1, scores, (lowest, lowest))
        m1 = jnp.max(m1, axis=1, keepdims=True)
        m2 = jnp.max(m2, axis=1, keepdims=True)

        def exps(j, carry):
            l1, l2 = carry
            p1 = jnp.exp2((p1s[j] - m1) * (SCALE * LOG2E))
            p2 = jnp.exp2((p2s[j] - m2) * (SCALE * LOG2E))
            p1s[j] = p1
            p2s[j] = p2
            return l1 + fold(jnp.add, p1), l2 + fold(jnp.add, p2)

        l1, l2 = lax.fori_loop(0, i + 1, exps, (zero128, zero128))
        inv1 = 1.0 / jnp.sum(l1, axis=1, keepdims=True)
        inv2 = 1.0 / jnp.sum(l2, axis=1, keepdims=True)
        winv2 = weight * inv2

        def mix(j, o):
            a = (p1s[j] * inv1 - p2s[j] * winv2).astype(jnp.bfloat16)
            mixs[j, rows, :] = a
            return o + dot_nn(a, vs[j].reshape(CHUNK, WIDTH))

        o = lax.fori_loop(0, i + 1, mix, jnp.zeros((TILE, WIDTH), jnp.float32))
        factor = lax.rsqrt(jnp.mean(o * o, axis=1, keepdims=True) + EPSILON)
        y = o * factor
        length = jnp.full((TILE, 1), lengths[4 * i], jnp.int32)
        for nl in range(1, 4):
            length = jnp.where(row // STRIPE == nl, lengths[4 * i + nl], length)
        live = (row_slot < length).astype(jnp.float32)
        g = qg[pl.ds(i * 4, 4), 1].reshape(TILE, WIDTH).astype(jnp.float32) * live
        d_out = (factor * (g - y * jnp.mean(g * y, axis=1, keepdims=True))).astype(jnp.bfloat16)

        def mix_grad(j, carry):
            e1, e2 = carry
            da = dot_nt(d_out, vs[j].reshape(CHUNK, WIDTH))
            das[j] = da
            return e1 + fold(jnp.add, da * p1s[j]), e2 + fold(jnp.add, da * p2s[j])

        e1, e2 = lax.fori_loop(0, i + 1, mix_grad, (zero128, zero128))
        e1 = jnp.sum(e1, axis=1, keepdims=True) * inv1
        e2 = jnp.sum(e2, axis=1, keepdims=True) * inv2

        def score_grad(j, carry):
            dq1, dq2 = carry
            da = das[j]
            t1 = (p1s[j] * (inv1 * (da - e1))).astype(jnp.bfloat16)
            t2 = (p2s[j] * (inv2 * (da - e2))).astype(jnp.bfloat16)
            t1s[j, rows, :] = t1
            t2s[j, rows, :] = t2
            k = ks[j].reshape(CHUNK, WIDTH)
            return dq1 + dot_nn(t1, k[:, :HALF]), dq2 + dot_nn(t2, k[:, HALF:])

        dq1, dq2 = lax.fori_loop(0, i + 1, score_grad, (zero128, zero128))
        return d_out, jnp.concatenate([dq1 * SCALE, dq2 * (-SCALE * weight)], axis=1)

    d_outs = []
    for i in range(GROUPS):
        d_out, dq = tile(i, None)
        d_outs.append(d_out)
        dq_out[4 * i : 4 * i + 4] = dq.astype(jnp.bfloat16).reshape(4, STRIPE, WIDTH)

    d_all = jnp.concatenate(d_outs, axis=0)
    q_all = qg[:, 0].reshape(ROWS, WIDTH)
    for j in range(GROUPS):
        lo = j * TILE
        for u in range(PARTS):
            cols = slice(u * TILE, (u + 1) * TILE)
            out = own_out if u < 4 else sib_out
            dk1 = dot_tn(t1s[j, lo:, cols], q_all[lo:, :HALF]) * SCALE
            dk2 = dot_tn(t2s[j, lo:, cols], q_all[lo:, HALF:]) * (-SCALE * weight)
            dv = dot_tn(mixs[j, lo:, cols], d_all[lo:])
            dk = jnp.concatenate([dk1, dk2], axis=1).astype(jnp.bfloat16)
            out[u % 4, 4 * j : 4 * j + 4, 0] = dk.reshape(4, STRIPE, WIDTH)
            out[u % 4, 4 * j : 4 * j + 4, 1] = dv.astype(jnp.bfloat16).reshape(4, STRIPE, WIDTH)


def core(lengths, where, lam, qg, kv_parts):
    vmem = pl.BlockSpec(memory_space=pltpu.VMEM)
    smem = pl.BlockSpec(memory_space=pltpu.SMEM)
    hbm = pl.BlockSpec(memory_space=pl.ANY)
    b16, f32 = jnp.bfloat16, jnp.float32
    return pl.pallas_call(
        core_kernel,
        out_shape=(
            jax.ShapeDtypeStruct((SLICES, STRIPE, WIDTH), b16),
            jax.ShapeDtypeStruct((4, SLICES, 2, STRIPE, WIDTH), b16),
            jax.ShapeDtypeStruct((4, SLICES, 2, STRIPE, WIDTH), b16),
        ),
        in_specs=[smem, smem, smem, vmem] + [hbm] * PARTS,
        out_specs=(vmem, vmem, vmem),
        scratch_shapes=[
            pltpu.VMEM((GROUPS, PARTS, 4, STRIPE, WIDTH), b16),
            pltpu.VMEM((GROUPS, PARTS, 4, STRIPE, WIDTH), b16),
            pltpu.VMEM((GROUPS, TILE, CHUNK), f32),
            pltpu.VMEM((GROUPS, TILE, CHUNK), f32),
            pltpu.VMEM((GROUPS, TILE, CHUNK), f32),
            pltpu.VMEM((GROUPS, ROWS, CHUNK), b16),
            pltpu.VMEM((GROUPS, ROWS, CHUNK), b16),
            pltpu.VMEM((GROUPS, ROWS, CHUNK), b16),
            pltpu.VMEM((GROUPS, 1, CHUNK), jnp.int32),
            pltpu.SemaphoreType.DMA((PARTS * 2 * GROUPS,)),
        ],
        compiler_params=pltpu.CompilerParams(vmem_limit_bytes=56 * 1024 * 1024),
        name="attention",
    )(lengths, where, lam, qg, *kv_parts)


def along_z(x, d):
    return lax.ppermute(x, "z", [(i, (i + d) % 4) for i in range(4)])


def swap(x):
    return lax.ppermute(x, "core", [(0, 1), (1, 0)])


def shards(queries, keys, values, out_grad, lam, lengths):
    z, c = lax.axis_index("z"), lax.axis_index("core")
    section = lax.axis_index("x") * 4 + lax.axis_index("y")

    kv = lax.all_to_all(pack(keys, values), SECTION, 0, 0, tiled=True)
    kv, qg_packed, lam = lax.optimization_barrier((kv, pack(queries, out_grad), lam))
    near = [kv] + [along_z(kv, d) for d in (1, 2, 3)]
    parts = near + [swap(x) for x in near]
    qg = lax.all_to_all(qg_packed, SECTION, 0, 0, tiled=True)
    lam_pad = jnp.broadcast_to(lam[None], (1, 2))
    lam_near = [lam_pad] + [along_z(lam_pad, d) for d in (1, 2, 3)]
    lams = jnp.concatenate(lam_near + [swap(x) for x in lam_near], axis=0)

    where = jnp.stack(
        [2 * ((z - d) % 4) + c for d in range(4)] + [2 * ((z - d) % 4) + 1 - c for d in range(4)]
    ).astype(jnp.int32)
    weight = jnp.sum(jnp.where((where == section // 2)[:, None], lams, 0.0), axis=0)
    weight = jnp.where(section % 2 == 0, weight[0], weight[1])

    d_query, own, sib = core(lengths, where, weight[None], qg, parts)

    f32, b16 = jnp.float32, jnp.bfloat16
    merged = (own.astype(f32) + swap(sib).astype(f32)).astype(b16)
    back = [along_z(merged[d], -d) for d in (1, 2, 3)]
    total = merged[0].astype(f32)
    for x in back:
        total = total + x.astype(f32)
    dq = lax.all_to_all(d_query, SECTION, 0, 0, tiled=True)
    dkv = lax.all_to_all(total.astype(b16), SECTION, 0, 0, tiled=True)
    dk, dv = unpack_pair(dkv)
    return (unpack_one(dq), dk, dv)


def solution(mesh):
    fine = Mesh(mesh.devices.reshape(4, 4, 4, 2), ("x", "y", "z", "core"))
    rows = P(("x", "y", "z", "core"), None)
    return jax.shard_map(
        shards,
        mesh=fine,
        in_specs=(rows, rows, rows, rows, P(("z", "core")), P()),
        out_specs=(rows, rows, rows),
        check_vma=False,
    )
```

```python
import functools

import jax
import jax.numpy as jnp
from jax import lax
from jax.experimental import pallas as pl
from jax.experimental.pallas import tpu as pltpu
from jax.sharding import Mesh
from jax.sharding import PartitionSpec as P

EPSILON = 1e-05
NEGATIVE = -1e30
LOG2E = 1.4426950408889634

STRIPE = 32
SLICES = 16
PARTS = 8
WIDTH = 256
HALF = 128
TILE = 128
GROUPS = 4
CHUNK = PARTS * TILE
ROWS = GROUPS * TILE
PAIRS = PARTS // 2
SECTION = ("x", "y")
ALL = ("x", "y", "z", "core")
SCALE = HALF ** (-0.5)


def pack_kernel(a_ref, b_ref, out_ref):
    for head in range(SLICES):
        cols = slice(head * WIDTH, (head + 1) * WIDTH)
        out_ref[head, 0] = a_ref[:, cols]
        out_ref[head, 1] = b_ref[:, cols]


def pack(a, b):
    return pl.pallas_call(
        pack_kernel,
        out_shape=jax.ShapeDtypeStruct((SLICES, 2, STRIPE, WIDTH), a.dtype),
        in_specs=[pl.BlockSpec(memory_space=pltpu.VMEM)] * 2,
        out_specs=pl.BlockSpec(memory_space=pltpu.VMEM),
        name="pack",
    )(a, b)


def unpack_pair_kernel(in_ref, a_ref, b_ref):
    for head in range(SLICES):
        cols = slice(head * WIDTH, (head + 1) * WIDTH)
        a_ref[:, cols] = in_ref[head, 0]
        b_ref[:, cols] = in_ref[head, 1]


def unpack_pair(x):
    shape = jax.ShapeDtypeStruct((STRIPE, SLICES * WIDTH), x.dtype)
    return pl.pallas_call(
        unpack_pair_kernel,
        out_shape=(shape, shape),
        in_specs=[pl.BlockSpec(memory_space=pltpu.VMEM)],
        out_specs=(pl.BlockSpec(memory_space=pltpu.VMEM),) * 2,
        name="unpack_pair",
    )(x)


def unpack_one_kernel(in_ref, a_ref):
    for head in range(SLICES):
        a_ref[:, head * WIDTH : (head + 1) * WIDTH] = in_ref[head]


def unpack_one(x):
    return pl.pallas_call(
        unpack_one_kernel,
        out_shape=jax.ShapeDtypeStruct((STRIPE, SLICES * WIDTH), x.dtype),
        in_specs=[pl.BlockSpec(memory_space=pltpu.VMEM)],
        out_specs=pl.BlockSpec(memory_space=pltpu.VMEM),
        name="unpack_one",
    )(x)


def dot_nt(a, b):
    return lax.dot_general(a, b, (((1,), (1,)), ((), ())), preferred_element_type=jnp.float32)


def dot_nn(a, b):
    return lax.dot_general(a, b, (((1,), (0,)), ((), ())), preferred_element_type=jnp.float32)


def dot_tn(a, b):
    return lax.dot_general(a, b, (((0,), (0,)), ((), ())), preferred_element_type=jnp.float32)


def fold(op, x):
    out = x[:, :128]
    for c in range(1, x.shape[1] // 128):
        out = op(out, x[:, c * 128 : (c + 1) * 128])
    return out


def core_kernel(lengths, where, lams, qg, *refs):
    kv_parts = refs[:PARTS]
    dq_out, *term_outs = refs[PARTS : PARTS + 1 + PARTS]
    ks, vs, p1s, p2s, das, mixs, t1s, t2s, outs, stat1, stat2, wide, key_pos, in_sems, out_sems = refs[
        2 * PARTS + 1 :
    ]

    copies = []
    for kind, dst in ((0, ks), (1, vs)):
        for u in range(PARTS):
            copy = pltpu.make_async_copy(
                kv_parts[u].at[:, :, kind], dst.at[:, u], in_sems.at[kind * PARTS + u]
            )
            copy.start()
            copies.append(copy)

    lane = lax.broadcasted_iota(jnp.int32, (1, TILE), 1)
    for j in range(GROUPS):
        length = jnp.full((1, TILE), lengths[4 * j], jnp.int32)
        for nl in range(1, 4):
            length = jnp.where(lane // STRIPE == nl, lengths[4 * j + nl], length)
        for u in range(PARTS):
            slot = where[u] * STRIPE + lane % STRIPE
            pos = 256 * (4 * j + lane // STRIPE) + slot
            key_pos[j, :, u * TILE : (u + 1) * TILE] = jnp.where(slot < length, pos, 1 << 30)

    weight = lams[where[PARTS] % 2]
    row = lax.broadcasted_iota(jnp.int32, (ROWS, 1), 0)
    row_slot = where[0] * STRIPE + row % STRIPE
    row_pos = 256 * (row // STRIPE) + row_slot
    q = qg[:, 0].reshape(ROWS, WIDTH)
    q1, q2 = q[:, :HALF], q[:, HALF:]
    stat1[...] = jnp.full((ROWS, 128), NEGATIVE, jnp.float32)
    stat2[...] = jnp.full((ROWS, 128), NEGATIVE, jnp.float32)

    for copy in copies[:PARTS]:
        copy.wait()
    for j in range(GROUPS):
        lo = j * TILE

        for pair in range(PAIRS):
            k = ks[j, slice(2 * pair, 2 * pair + 2)].reshape(2 * TILE, WIDTH)
            cols = slice(pair * 2 * TILE, (pair + 1) * 2 * TILE)
            vis = key_pos[j, :, cols] <= row_pos[lo:]
            s1 = jnp.where(vis, dot_nt(q1[lo:], k[:, :HALF]), NEGATIVE)
            s2 = jnp.where(vis, dot_nt(q2[lo:], k[:, HALF:]), NEGATIVE)
            p1s[j, lo:, cols] = s1
            p2s[j, lo:, cols] = s2
            stat1[lo:] = jnp.maximum(stat1[lo:], fold(jnp.maximum, s1))
            stat2[lo:] = jnp.maximum(stat2[lo:], fold(jnp.maximum, s2))

    m1 = jnp.max(stat1[...], axis=1, keepdims=True)
    m2 = jnp.max(stat2[...], axis=1, keepdims=True)
    stat1[...] = jnp.zeros((ROWS, 128), jnp.float32)
    stat2[...] = jnp.zeros((ROWS, 128), jnp.float32)
    for j in range(GROUPS):
        lo = j * TILE

        for pair in range(PAIRS):
            cols = slice(pair * 2 * TILE, (pair + 1) * 2 * TILE)
            p1 = jnp.exp2((p1s[j, lo:, cols] - m1[lo:]) * (SCALE * LOG2E))
            p2 = jnp.exp2((p2s[j, lo:, cols] - m2[lo:]) * (SCALE * LOG2E))
            p1s[j, lo:, cols] = p1
            p2s[j, lo:, cols] = p2
            stat1[lo:] += fold(jnp.add, p1)
            stat2[lo:] += fold(jnp.add, p2)

    inv1 = 1.0 / jnp.sum(stat1[...], axis=1, keepdims=True)
    inv2 = 1.0 / jnp.sum(stat2[...], axis=1, keepdims=True)
    winv2 = weight * inv2

    for copy in copies[PARTS:]:
        copy.wait()
    wide[...] = jnp.zeros((ROWS, WIDTH), jnp.float32)
    for j in range(GROUPS):
        lo = j * TILE

        for pair in range(PAIRS):
            cols = slice(pair * 2 * TILE, (pair + 1) * 2 * TILE)
            a = p1s[j, lo:, cols] * inv1[lo:] - p2s[j, lo:, cols] * winv2[lo:]
            mixs[j, lo:, cols] = a.astype(jnp.bfloat16)

        wide[lo:] += dot_nn(mixs[j, lo:], vs[j].reshape(CHUNK, WIDTH))

    o = wide[...]
    factor = lax.rsqrt(jnp.mean(o * o, axis=1, keepdims=True) + EPSILON)
    y = o * factor
    length = jnp.full((ROWS, 1), lengths[0], jnp.int32)
    for n in range(1, SLICES):
        length = jnp.where(row // STRIPE == n, lengths[n], length)
    live = (row_slot < length).astype(jnp.float32)
    g = qg[:, 1].reshape(ROWS, WIDTH).astype(jnp.float32) * live
    d_out = (factor * (g - y * jnp.mean(g * y, axis=1, keepdims=True))).astype(jnp.bfloat16)

    stat1[...] = jnp.zeros((ROWS, 128), jnp.float32)
    stat2[...] = jnp.zeros((ROWS, 128), jnp.float32)
    for j in range(GROUPS):
        lo = j * TILE

        for pair in range(PAIRS):
            cols = slice(pair * 2 * TILE, (pair + 1) * 2 * TILE)
            da = dot_nt(d_out[lo:], vs[j, slice(2 * pair, 2 * pair + 2)].reshape(2 * TILE, WIDTH))
            das[j, lo:, cols] = da
            stat1[lo:] += fold(jnp.add, da * p1s[j, lo:, cols])
            stat2[lo:] += fold(jnp.add, da * p2s[j, lo:, cols])

    e1 = jnp.sum(stat1[...], axis=1, keepdims=True) * inv1
    e2 = jnp.sum(stat2[...], axis=1, keepdims=True) * inv2

    wide[...] = jnp.zeros((ROWS, WIDTH), jnp.float32)
    out_copies = []
    for j in range(GROUPS):
        lo = j * TILE

        for pair in range(PAIRS):
            cols = slice(pair * 2 * TILE, (pair + 1) * 2 * TILE)
            da = das[j, lo:, cols]
            t1 = p1s[j, lo:, cols] * (inv1[lo:] * (da - e1[lo:]))
            t2 = p2s[j, lo:, cols] * (inv2[lo:] * (da - e2[lo:]))
            t1s[j, lo:, cols] = t1.astype(jnp.bfloat16)
            t2s[j, lo:, cols] = t2.astype(jnp.bfloat16)

        k = ks[j].reshape(CHUNK, WIDTH)
        wide[lo:, :HALF] += dot_nn(t1s[j, lo:], k[:, :HALF])
        wide[lo:, HALF:] += dot_nn(t2s[j, lo:], k[:, HALF:])

        for pair in range(PAIRS):
            cols = slice(pair * 2 * TILE, (pair + 1) * 2 * TILE)
            dk1 = dot_tn(t1s[j, lo:, cols], q1[lo:]) * SCALE
            dk2 = dot_tn(t2s[j, lo:, cols], q2[lo:]) * (-SCALE * weight)
            dv = dot_tn(mixs[j, lo:, cols], d_out[lo:]).astype(jnp.bfloat16)
            dk = jnp.concatenate([dk1, dk2], axis=1).astype(jnp.bfloat16)
            outs[j, slice(2 * pair, 2 * pair + 2), :, 0] = dk.reshape(2, 4, STRIPE, WIDTH)
            outs[j, slice(2 * pair, 2 * pair + 2), :, 1] = dv.reshape(2, 4, STRIPE, WIDTH)

        for u in range(PARTS):
            copy = pltpu.make_async_copy(
                outs.at[j, u], term_outs[u].at[pl.ds(4 * j, 4)], out_sems.at[PARTS * j + u]
            )
            copy.start()
            out_copies.append(copy)

    dq_out[:, :, :HALF] = (wide[:, :HALF] * SCALE).astype(jnp.bfloat16).reshape(SLICES, STRIPE, HALF)
    dq_out[:, :, HALF:] = (
        (wide[:, HALF:] * (-SCALE * weight)).astype(jnp.bfloat16).reshape(SLICES, STRIPE, HALF)
    )
    for copy in out_copies:
        copy.wait()


def core(lengths, where, lams, qg, kv_parts):
    vmem = pl.BlockSpec(memory_space=pltpu.VMEM)
    smem = pl.BlockSpec(memory_space=pltpu.SMEM)
    hbm = pl.BlockSpec(memory_space=pl.ANY)
    b16, f32 = jnp.bfloat16, jnp.float32
    parts = [x.reshape(GROUPS, 4, 2, STRIPE, WIDTH) for x in kv_parts]
    return pl.pallas_call(
        core_kernel,
        out_shape=(
            jax.ShapeDtypeStruct((SLICES, STRIPE, WIDTH), b16),
        )
        + (jax.ShapeDtypeStruct((SLICES, 2, STRIPE, WIDTH), b16),) * PARTS,
        in_specs=[smem, smem, smem, vmem] + [hbm] * PARTS,
        out_specs=(vmem,) + (hbm,) * PARTS,
        scratch_shapes=[
            pltpu.VMEM((GROUPS, PARTS, 4, STRIPE, WIDTH), b16),
            pltpu.VMEM((GROUPS, PARTS, 4, STRIPE, WIDTH), b16),
            pltpu.VMEM((GROUPS, ROWS, CHUNK), f32),
            pltpu.VMEM((GROUPS, ROWS, CHUNK), f32),
            pltpu.VMEM((GROUPS, ROWS, CHUNK), f32),
            pltpu.VMEM((GROUPS, ROWS, CHUNK), b16),
            pltpu.VMEM((GROUPS, ROWS, CHUNK), b16),
            pltpu.VMEM((GROUPS, ROWS, CHUNK), b16),
            pltpu.VMEM((GROUPS, PARTS, 4, 2, STRIPE, WIDTH), b16),
            pltpu.VMEM((ROWS, 128), f32),
            pltpu.VMEM((ROWS, 128), f32),
            pltpu.VMEM((ROWS, WIDTH), f32),
            pltpu.VMEM((GROUPS, 1, CHUNK), jnp.int32),
            pltpu.SemaphoreType.DMA((PARTS * 2,)),
            pltpu.SemaphoreType.DMA((GROUPS * PARTS,)),
        ],
        compiler_params=pltpu.CompilerParams(vmem_limit_bytes=60 * 1024 * 1024),
        name="attention",
    )(lengths, where, lams, qg, *parts)


def along_z(x, d):
    return lax.ppermute(x, "z", [(i, (i + d) % 4) for i in range(4)])


def swap(x):
    return lax.ppermute(x, "core", [(0, 1), (1, 0)])


def shards(queries, keys, values, out_grad, lam, lengths):
    z, c = lax.axis_index("z"), lax.axis_index("core")
    section = lax.axis_index("x") * 4 + lax.axis_index("y")
    where = jnp.stack(
        [2 * ((z - d) % 4) + c for d in range(4)]
        + [2 * ((z - d) % 4) + 1 - c for d in range(4)]
        + [section]
    ).astype(jnp.int32)

    kv = lax.all_to_all(pack(keys, values), SECTION, 0, 0, tiled=True)
    lams = lax.ppermute(
        lam, ALL, [(s * 8 + t, (2 * t + s // 8) * 8 + s % 8) for s in range(SLICES) for t in range(PARTS)]
    )
    kv, qg, lams = lax.optimization_barrier((kv, pack(queries, out_grad), lams))
    near = [along_z(kv, d) for d in (1, 2, 3)]
    qg = lax.all_to_all(qg, SECTION, 0, 0, tiled=True)
    *near, qg = lax.optimization_barrier((*near, qg))
    near = [kv] + near

    d_query, *terms = core(lengths, where, lams, qg, near + [swap(x) for x in near])

    f32, b16 = jnp.float32, jnp.bfloat16
    dq = lax.all_to_all(d_query, SECTION, 0, 0, tiled=True)
    merged = [
        (own.astype(f32) + swap(other).astype(f32)).astype(b16)
        for own, other in zip(terms[:4], terms[4:])
    ]
    total = merged[0].astype(f32)
    for d in (1, 2, 3):
        total = total + along_z(merged[d], -d).astype(f32)
    dkv = lax.all_to_all(total.astype(b16), SECTION, 0, 0, tiled=True)
    dk, dv = unpack_pair(dkv)
    return (unpack_one(dq), dk, dv)


def solution(mesh):
    fine = Mesh(mesh.devices.reshape(4, 4, 4, 2), ("x", "y", "z", "core"))
    rows = P(ALL, None)
    return jax.shard_map(
        shards,
        mesh=fine,
        in_specs=(rows, rows, rows, rows, P(("z", "core")), P()),
        out_specs=(rows, rows, rows),
        check_vma=False,
    )
```

```python
import functools

import jax
import jax.numpy as jnp
from jax import lax
from jax.experimental import pallas as pl
from jax.experimental.pallas import tpu as pltpu
from jax.sharding import Mesh
from jax.sharding import PartitionSpec as P

EPSILON = 1e-05
NEGATIVE = -1e30
LOG2E = 1.4426950408889634

STRIPE = 32
SLICES = 16
PARTS = 8
WIDTH = 256
HALF = 128
TILE = 128
GROUPS = 4
CHUNK = PARTS * TILE
ROWS = GROUPS * TILE
PAIRS = PARTS // 2
LIVE_PAIRS = 2
SECTION = ("x", "y")
ALL = ("x", "y", "z", "core")
SCALE = HALF ** (-0.5)


def pack_kernel(a_ref, b_ref, out_ref):
    for head in range(SLICES):
        cols = slice(head * WIDTH, (head + 1) * WIDTH)
        out_ref[head, 0] = a_ref[:, cols]
        out_ref[head, 1] = b_ref[:, cols]


def pack(a, b):
    return pl.pallas_call(
        pack_kernel,
        out_shape=jax.ShapeDtypeStruct((SLICES, 2, STRIPE, WIDTH), a.dtype),
        in_specs=[pl.BlockSpec(memory_space=pltpu.VMEM)] * 2,
        out_specs=pl.BlockSpec(memory_space=pltpu.VMEM),
        name="pack",
    )(a, b)


def unpack_kernel(in_ref, *outs):
    for head in range(SLICES):
        for i, out in enumerate(outs):
            out[:, head * WIDTH : (head + 1) * WIDTH] = in_ref[head, i]


def unpack(x):
    shape = jax.ShapeDtypeStruct((STRIPE, SLICES * WIDTH), x.dtype)
    return pl.pallas_call(
        unpack_kernel,
        out_shape=(shape,) * 3,
        in_specs=[pl.BlockSpec(memory_space=pltpu.VMEM)],
        out_specs=(pl.BlockSpec(memory_space=pltpu.VMEM),) * 3,
        name="unpack",
    )(x)


def dot_nt(a, b):
    return lax.dot_general(a, b, (((1,), (1,)), ((), ())), preferred_element_type=jnp.float32)


def dot_nn(a, b):
    return lax.dot_general(a, b, (((1,), (0,)), ((), ())), preferred_element_type=jnp.float32)


def dot_tn(a, b):
    return lax.dot_general(a, b, (((0,), (0,)), ((), ())), preferred_element_type=jnp.float32)


def fold(op, x):
    out = x[:, :128]
    for c in range(1, x.shape[1] // 128):
        out = op(out, x[:, c * 128 : (c + 1) * 128])
    return out


def core_kernel(lengths, where, lams, qg, *refs):
    kv_halves = refs[: 2 * PARTS]
    dq_out, *term_outs = refs[2 * PARTS : 4 * PARTS + 1]
    ks, vs, p1s, p2s, das, mixs, t1s, t2s, outs, stat1, stat2, wide, in_sems, out_sems = refs[
        4 * PARTS + 1 :
    ]

    copies = []
    for kind, dst in ((0, ks), (1, vs)):
        for half in range(2):
            for u in range(PARTS):
                copy = pltpu.make_async_copy(
                    kv_halves[2 * u + half].at[:, :, kind],
                    dst.at[2 * half : 2 * half + 2, where[u]],
                    in_sems.at[(kind * 2 + half) * PARTS + u],
                )
                copy.start()
                copies.append(copy)

    lane = lax.broadcasted_iota(jnp.int32, (1, 2 * TILE), 1)
    lane_slice = lane % TILE // STRIPE

    weight = lams[where[PARTS] % 2]
    row = lax.broadcasted_iota(jnp.int32, (ROWS, 1), 0)
    row_slot = where[0] * STRIPE + row % STRIPE
    tile_pos = 256 * (row[:TILE] // STRIPE) + row_slot[:TILE]
    q = qg[:, 0].reshape(ROWS, WIDTH)
    q1, q2 = q[:, :HALF], q[:, HALF:]
    stat1[...] = jnp.full((ROWS, 128), NEGATIVE, jnp.float32)
    stat2[...] = jnp.full((ROWS, 128), NEGATIVE, jnp.float32)

    for j in range(GROUPS):
        lo = j * TILE
        if j % 2 == 0:
            for copy in copies[j // 2 * PARTS : (j // 2 + 1) * PARTS]:
                copy.wait()

        for pair in range(PAIRS):
            k = ks[j, slice(2 * pair, 2 * pair + 2)].reshape(2 * TILE, WIDTH)
            cols = slice(pair * 2 * TILE, (pair + 1) * 2 * TILE)
            slot = (2 * pair + lane // TILE) * STRIPE + lane % STRIPE
            vis = 256 * lane_slice + slot <= tile_pos
            if pair >= LIVE_PAIRS:
                length = jnp.full((1, 2 * TILE), lengths[4 * j], jnp.int32)
                for nl in range(1, 4):
                    length = jnp.where(lane_slice == nl, lengths[4 * j + nl], length)
                vis = vis & (slot < length)
                hide = jnp.where(slot < length, 0.0, NEGATIVE)
            for half, p, stat in ((0, p1s, stat1), (HALF, p2s, stat2)):
                scores = dot_nt(q[lo:, half : half + HALF], k[:, half : half + HALF])
                top, rest = jnp.where(vis, scores[:TILE], NEGATIVE), scores[TILE:]
                p[j, lo : lo + TILE, cols] = top
                stat[lo : lo + TILE] = jnp.maximum(stat[lo : lo + TILE], fold(jnp.maximum, top))
                if j < GROUPS - 1:
                    rest = rest + hide if pair >= LIVE_PAIRS else rest
                    p[j, lo + TILE :, cols] = rest
                    stat[lo + TILE :] = jnp.maximum(stat[lo + TILE :], fold(jnp.maximum, rest))

    m1 = jnp.max(stat1[...], axis=1, keepdims=True)
    m2 = jnp.max(stat2[...], axis=1, keepdims=True)
    stat1[...] = jnp.zeros((ROWS, 128), jnp.float32)
    stat2[...] = jnp.zeros((ROWS, 128), jnp.float32)
    for j in range(GROUPS):
        lo = j * TILE

        for pair in range(PAIRS):
            cols = slice(pair * 2 * TILE, (pair + 1) * 2 * TILE)
            p1 = jnp.exp2((p1s[j, lo:, cols] - m1[lo:]) * (SCALE * LOG2E))
            p2 = jnp.exp2((p2s[j, lo:, cols] - m2[lo:]) * (SCALE * LOG2E))
            p1s[j, lo:, cols] = p1
            p2s[j, lo:, cols] = p2
            stat1[lo:] += fold(jnp.add, p1)
            stat2[lo:] += fold(jnp.add, p2)

    inv1 = 1.0 / jnp.sum(stat1[...], axis=1, keepdims=True)
    inv2 = 1.0 / jnp.sum(stat2[...], axis=1, keepdims=True)
    winv2 = weight * inv2

    for copy in copies[2 * PARTS :]:
        copy.wait()
    wide[...] = jnp.zeros((ROWS, WIDTH), jnp.float32)
    for j in range(GROUPS):
        lo = j * TILE

        for pair in range(PAIRS):
            cols = slice(pair * 2 * TILE, (pair + 1) * 2 * TILE)
            a = p1s[j, lo:, cols] * inv1[lo:] - p2s[j, lo:, cols] * winv2[lo:]
            mixs[j, lo:, cols] = a.astype(jnp.bfloat16)

        wide[lo:] += dot_nn(mixs[j, lo:], vs[j].reshape(CHUNK, WIDTH))

    o = wide[...]
    factor = lax.rsqrt(jnp.mean(o * o, axis=1, keepdims=True) + EPSILON)
    y = o * factor
    length = jnp.full((ROWS, 1), lengths[0], jnp.int32)
    for n in range(1, SLICES):
        length = jnp.where(row // STRIPE == n, lengths[n], length)
    live = (row_slot < length).astype(jnp.float32)
    g = qg[:, 1].reshape(ROWS, WIDTH).astype(jnp.float32) * live
    d_out = (factor * (g - y * jnp.mean(g * y, axis=1, keepdims=True))).astype(jnp.bfloat16)

    stat1[...] = jnp.zeros((ROWS, 128), jnp.float32)
    stat2[...] = jnp.zeros((ROWS, 128), jnp.float32)
    for j in range(GROUPS):
        lo = j * TILE

        for pair in range(PAIRS):
            cols = slice(pair * 2 * TILE, (pair + 1) * 2 * TILE)
            da = dot_nt(d_out[lo:], vs[j, slice(2 * pair, 2 * pair + 2)].reshape(2 * TILE, WIDTH))
            das[j, lo:, cols] = da
            stat1[lo:] += fold(jnp.add, da * p1s[j, lo:, cols])
            stat2[lo:] += fold(jnp.add, da * p2s[j, lo:, cols])

    e1 = jnp.sum(stat1[...], axis=1, keepdims=True) * inv1
    e2 = jnp.sum(stat2[...], axis=1, keepdims=True) * inv2

    wide[...] = jnp.zeros((ROWS, WIDTH), jnp.float32)
    out_copies = []
    for j in range(GROUPS):
        lo = j * TILE

        for pair in range(PAIRS):
            cols = slice(pair * 2 * TILE, (pair + 1) * 2 * TILE)
            da = das[j, lo:, cols]
            t1 = p1s[j, lo:, cols] * (inv1[lo:] * (da - e1[lo:]))
            t2 = p2s[j, lo:, cols] * (inv2[lo:] * (da - e2[lo:]))
            t1s[j, lo:, cols] = t1.astype(jnp.bfloat16)
            t2s[j, lo:, cols] = t2.astype(jnp.bfloat16)

        k = ks[j].reshape(CHUNK, WIDTH)
        wide[lo:, :HALF] += dot_nn(t1s[j, lo:], k[:, :HALF])
        wide[lo:, HALF:] += dot_nn(t2s[j, lo:], k[:, HALF:])

        for pair in range(PAIRS):
            cols = slice(pair * 2 * TILE, (pair + 1) * 2 * TILE)
            dk1 = dot_tn(t1s[j, lo:, cols], q1[lo:]) * SCALE
            dk2 = dot_tn(t2s[j, lo:, cols], q2[lo:]) * (-SCALE * weight)
            dv = dot_tn(mixs[j, lo:, cols], d_out[lo:]).astype(jnp.bfloat16)
            dk = jnp.concatenate([dk1, dk2], axis=1).astype(jnp.bfloat16)
            outs[j, slice(2 * pair, 2 * pair + 2), :, 0] = dk.reshape(2, 4, STRIPE, WIDTH)
            outs[j, slice(2 * pair, 2 * pair + 2), :, 1] = dv.reshape(2, 4, STRIPE, WIDTH)

        for u in range(PARTS):
            copy = pltpu.make_async_copy(
                outs.at[j, where[u]],
                term_outs[2 * u + j // 2].at[4 * (j % 2) : 4 * (j % 2) + 4],
                out_sems.at[PARTS * j + u],
            )
            copy.start()
            out_copies.append(copy)

    dq_out[:, :, :HALF] = (wide[:, :HALF] * SCALE).astype(jnp.bfloat16).reshape(SLICES, STRIPE, HALF)
    dq_out[:, :, HALF:] = (
        (wide[:, HALF:] * (-SCALE * weight)).astype(jnp.bfloat16).reshape(SLICES, STRIPE, HALF)
    )
    for copy in out_copies:
        copy.wait()


def core(lengths, where, lams, qg, kv_halves):
    vmem = pl.BlockSpec(memory_space=pltpu.VMEM)
    smem = pl.BlockSpec(memory_space=pltpu.SMEM)
    hbm = pl.BlockSpec(memory_space=pl.ANY)
    b16, f32 = jnp.bfloat16, jnp.float32
    halves = [x.reshape(2, 4, 2, STRIPE, WIDTH) for x in kv_halves]
    return pl.pallas_call(
        core_kernel,
        out_shape=(
            jax.ShapeDtypeStruct((SLICES, STRIPE, WIDTH), b16),
        )
        + (jax.ShapeDtypeStruct((SLICES // 2, 2, STRIPE, WIDTH), b16),) * (2 * PARTS),
        in_specs=[smem, smem, smem, vmem] + [hbm] * (2 * PARTS),
        out_specs=(vmem,) + (hbm,) * (2 * PARTS),
        scratch_shapes=[
            pltpu.VMEM((GROUPS, PARTS, 4, STRIPE, WIDTH), b16),
            pltpu.VMEM((GROUPS, PARTS, 4, STRIPE, WIDTH), b16),
            pltpu.VMEM((GROUPS, ROWS, CHUNK), f32),
            pltpu.VMEM((GROUPS, ROWS, CHUNK), f32),
            pltpu.VMEM((GROUPS, ROWS, CHUNK), f32),
            pltpu.VMEM((GROUPS, ROWS, CHUNK), b16),
            pltpu.VMEM((GROUPS, ROWS, CHUNK), b16),
            pltpu.VMEM((GROUPS, ROWS, CHUNK), b16),
            pltpu.VMEM((GROUPS, PARTS, 4, 2, STRIPE, WIDTH), b16),
            pltpu.VMEM((ROWS, 128), f32),
            pltpu.VMEM((ROWS, 128), f32),
            pltpu.VMEM((ROWS, WIDTH), f32),
            pltpu.SemaphoreType.DMA((PARTS * 4,)),
            pltpu.SemaphoreType.DMA((GROUPS * PARTS,)),
        ],
        compiler_params=pltpu.CompilerParams(vmem_limit_bytes=60 * 1024 * 1024),
        name="attention",
    )(lengths, where, lams, qg, *halves)


def final_kernel(*refs):
    d_query, *ins, out = refs
    out[:, 0] = d_query[...]
    for half in range(2):
        total = ins[half][...].astype(jnp.float32)
        for x in ins[2 + half :: 2]:
            total = total + x[...].astype(jnp.float32)
        out[8 * half : 8 * half + 8, 1:] = total.astype(out.dtype)


def final(d_query, *halves):
    return pl.pallas_call(
        final_kernel,
        out_shape=jax.ShapeDtypeStruct((SLICES, 3, STRIPE, WIDTH), jnp.bfloat16),
        in_specs=[pl.BlockSpec(memory_space=pltpu.VMEM)] * (1 + len(halves)),
        out_specs=pl.BlockSpec(memory_space=pltpu.VMEM),
        name="final",
    )(d_query, *halves)


def along_z(x, d):
    return lax.ppermute(x, "z", [(i, (i + d) % 4) for i in range(4)])


def swap(x):
    return lax.ppermute(x, "core", [(0, 1), (1, 0)])


def shards(queries, keys, values, out_grad, lam, lengths):
    z, c = lax.axis_index("z"), lax.axis_index("core")
    section = lax.axis_index("x") * 4 + lax.axis_index("y")
    where = jnp.stack(
        [2 * ((z - d) % 4) + c for d in range(4)]
        + [2 * ((z - d) % 4) + 1 - c for d in range(4)]
        + [section]
    ).astype(jnp.int32)

    kv = lax.all_to_all(pack(keys, values), SECTION, 0, 0, tiled=True)
    lams = lax.ppermute(
        lam, ALL, [(s * 8 + t, (2 * t + s // 8) * 8 + s % 8) for s in range(SLICES) for t in range(PARTS)]
    )
    kv, qg, lams = lax.optimization_barrier((kv, pack(queries, out_grad), lams))
    lower, upper = lax.optimization_barrier((kv[:8], kv[8:]))
    lower_up, upper_down = along_z(lower, 1), along_z(upper, -1)
    upper_up, lower_down = along_z(upper, 1), along_z(lower, -1)
    lower_far, upper_far = along_z(lower_up, 1), along_z(upper_down, -1)
    qg = lax.all_to_all(qg, SECTION, 0, 0, tiled=True)
    upper_up, lower_down, qg = lax.optimization_barrier((upper_up, lower_down, qg))
    near = [lower, upper, lower_up, upper_up, lower_far, upper_far, lower_down, upper_down]

    d_query, *terms = core(lengths, where, lams, qg, near + [swap(x) for x in near])

    def add(*xs):
        return sum(x.astype(jnp.float32) for x in xs).astype(jnp.bfloat16)

    own, other = terms[:PARTS], [swap(x) for x in terms[PARTS:]]
    lower_far = along_z(add(own[4], other[4]), -1)
    upper_far = along_z(add(own[5], other[5]), 1)
    upper_1 = along_z(add(own[3], other[3]), -1)
    lower_3 = along_z(add(own[6], other[6]), 1)
    lower_1 = along_z(add(own[2], other[2], lower_far), -1)
    upper_3 = along_z(add(own[7], other[7], upper_far), 1)
    total = final(d_query, own[0], own[1], other[0], other[1], lower_3, upper_1, lower_1, upper_3)
    return unpack(lax.all_to_all(total, SECTION, 0, 0, tiled=True))


def solution(mesh):
    fine = Mesh(mesh.devices.reshape(4, 4, 4, 2), ("x", "y", "z", "core"))
    rows = P(ALL, None)
    return jax.shard_map(
        shards,
        mesh=fine,
        in_specs=(rows, rows, rows, rows, P(("z", "core")), P()),
        out_specs=(rows, rows, rows),
        check_vma=False,
    )
```

```python
import functools

import jax
import jax.numpy as jnp
from jax import lax
from jax.experimental import pallas as pl
from jax.experimental.pallas import tpu as pltpu
from jax.sharding import Mesh
from jax.sharding import PartitionSpec as P

EPSILON = 1e-05
NEGATIVE = -1e30
LOG2E = 1.4426950408889634

STRIPE = 32
SLICES = 16
PARTS = 8
WIDTH = 256
HALF = 128
ROWS = SLICES * STRIPE
TILE = 64
NEXT = TILE // STRIPE
GROUPS = ROWS // TILE
CHUNK = PARTS * TILE
STORED = sum(ROWS - j * TILE for j in range(GROUPS))
STEP = 256
SPAN = STEP // TILE
STEPS = PARTS // SPAN
HALVES = GROUPS // 2
LIVE_STEPS = STEPS // 2
SECTION = ("x", "y")
ALL = ("x", "y", "z", "core")
SCALE = HALF ** (-0.5)


def pack_kernel(a_ref, b_ref, out_ref):
    for head in range(SLICES):
        cols = slice(head * WIDTH, (head + 1) * WIDTH)
        out_ref[head, 0] = a_ref[:, cols]
        out_ref[head, 1] = b_ref[:, cols]


def pack(a, b):
    return pl.pallas_call(
        pack_kernel,
        out_shape=jax.ShapeDtypeStruct((SLICES, 2, STRIPE, WIDTH), a.dtype),
        in_specs=[pl.BlockSpec(memory_space=pltpu.VMEM)] * 2,
        out_specs=pl.BlockSpec(memory_space=pltpu.VMEM),
        name="pack",
    )(a, b)


def unpack_kernel(in_ref, *outs):
    for head in range(SLICES):
        for i, out in enumerate(outs):
            out[:, head * WIDTH : (head + 1) * WIDTH] = in_ref[head, i]


def unpack(x):
    shape = jax.ShapeDtypeStruct((STRIPE, SLICES * WIDTH), x.dtype)
    return pl.pallas_call(
        unpack_kernel,
        out_shape=(shape,) * 3,
        in_specs=[pl.BlockSpec(memory_space=pltpu.VMEM)],
        out_specs=(pl.BlockSpec(memory_space=pltpu.VMEM),) * 3,
        name="unpack",
    )(x)


def dot_nt(a, b):
    return lax.dot_general(a, b, (((1,), (1,)), ((), ())), preferred_element_type=jnp.float32)


def dot_nn(a, b):
    return lax.dot_general(a, b, (((1,), (0,)), ((), ())), preferred_element_type=jnp.float32)


def dot_tn(a, b):
    return lax.dot_general(a, b, (((0,), (0,)), ((), ())), preferred_element_type=jnp.float32)


def fold(op, x):
    out = x[:, :128]
    for c in range(1, x.shape[1] // 128):
        out = op(out, x[:, c * 128 : (c + 1) * 128])
    return out


def core_kernel(lengths, where, lams, qg_in, *refs):
    kv_halves = refs[: 2 * PARTS]
    dq_out, *term_outs = refs[2 * PARTS : 4 * PARTS + 1]
    qg, dq, kvs, p1s, p2s, das, mixs, t1s, t2s, outs, stat1, stat2, wide, dos, in_sems, out_sems = refs[
        4 * PARTS + 1 :
    ]

    copies = {}

    def fetch(name, src, dst):
        copy = pltpu.make_async_copy(src, dst, in_sems.at[sum(map(len, copies.values()))])
        copy.start()
        copies.setdefault(name, []).append(copy)

    def arrived(*name):
        for copy in copies[name]:
            copy.wait()

    fetch(("queries",), qg_in, qg)
    for kind in range(2):
        for half in range(2):
            for u in range(PARTS):
                chunks = slice(half * HALVES, (half + 1) * HALVES)
                fetch((kind, half), kv_halves[2 * u + half].at[:, :, kind], kvs.at[chunks, where[u], :, kind])

    def keys(j, parts=slice(0, PARTS)):
        return kvs[j, parts, :, 0].reshape(-1, WIDTH)

    def values(j, parts=slice(0, PARTS)):
        return kvs[j, parts, :, 1].reshape(-1, WIDTH)

    def of(j, skip=0, count=None):
        first = sum(ROWS - i * TILE for i in range(j)) + skip
        return slice(first, first + (ROWS - j * TILE - skip if count is None else count))

    lane = lax.broadcasted_iota(jnp.int32, (1, STEP), 1)
    lane_slice = lane % TILE // STRIPE

    weight = lams[where[PARTS] % 2]
    row = lax.broadcasted_iota(jnp.int32, (ROWS, 1), 0)
    row_slot = where[0] * STRIPE + row % STRIPE
    tile_pos = 256 * (row[:TILE] // STRIPE) + row_slot[:TILE]
    arrived("queries")
    q = qg[:, 0].reshape(ROWS, WIDTH)
    q1, q2 = q[:, :HALF], q[:, HALF:]
    stat1[...] = jnp.full((ROWS, 128), NEGATIVE, jnp.float32)
    stat2[...] = jnp.full((ROWS, 128), NEGATIVE, jnp.float32)

    for j in range(GROUPS):
        lo = j * TILE
        if j % HALVES == 0:
            arrived(0, j // HALVES)

        for step in range(STEPS):
            k = keys(j, slice(SPAN * step, SPAN * step + SPAN))
            cols = slice(step * STEP, (step + 1) * STEP)
            slot = (SPAN * step + lane // TILE) * STRIPE + lane % STRIPE
            vis = 256 * lane_slice + slot <= tile_pos
            if step >= LIVE_STEPS:
                length = jnp.full((1, STEP), lengths[NEXT * j], jnp.int32)
                for nl in range(1, NEXT):
                    length = jnp.where(lane_slice == nl, lengths[NEXT * j + nl], length)
                vis = vis & (slot < length)
                hide = jnp.where(slot < length, 0.0, NEGATIVE)
            for half, p, stat in ((0, p1s, stat1), (HALF, p2s, stat2)):
                scores = dot_nt(q[lo:, half : half + HALF], k[:, half : half + HALF])
                top, rest = jnp.where(vis, scores[:TILE], NEGATIVE), scores[TILE:]
                p[of(j, 0, TILE), cols] = top
                stat[lo : lo + TILE] = jnp.maximum(stat[lo : lo + TILE], fold(jnp.maximum, top))
                if j < GROUPS - 1:
                    rest = rest + hide if step >= LIVE_STEPS else rest
                    p[of(j, TILE), cols] = rest
                    stat[lo + TILE :] = jnp.maximum(stat[lo + TILE :], fold(jnp.maximum, rest))

    m1 = jnp.max(stat1[...], axis=1, keepdims=True)
    m2 = jnp.max(stat2[...], axis=1, keepdims=True)
    stat1[...] = jnp.zeros((ROWS, 128), jnp.float32)
    stat2[...] = jnp.zeros((ROWS, 128), jnp.float32)
    for j in range(GROUPS):
        lo = j * TILE

        for step in range(STEPS):
            cols = slice(step * STEP, (step + 1) * STEP)
            p1 = jnp.exp2((p1s[of(j), cols] - m1[lo:]) * (SCALE * LOG2E))
            p2 = jnp.exp2((p2s[of(j), cols] - m2[lo:]) * (SCALE * LOG2E))
            p1s[of(j), cols] = p1
            p2s[of(j), cols] = p2
            stat1[lo:] += fold(jnp.add, p1)
            stat2[lo:] += fold(jnp.add, p2)

    inv1 = 1.0 / jnp.sum(stat1[...], axis=1, keepdims=True)
    inv2 = 1.0 / jnp.sum(stat2[...], axis=1, keepdims=True)
    winv2 = weight * inv2

    wide[...] = jnp.zeros((ROWS, WIDTH), jnp.float32)
    for j in range(GROUPS):
        lo = j * TILE
        if j % HALVES == 0:
            arrived(1, j // HALVES)

        for step in range(STEPS):
            cols = slice(step * STEP, (step + 1) * STEP)
            a = p1s[of(j), cols] * inv1[lo:] - p2s[of(j), cols] * winv2[lo:]
            mixs[of(j), cols] = a.astype(jnp.bfloat16)

        wide[lo:] += dot_nn(mixs[of(j)], values(j))

    for n in range(SLICES):
        part = slice(n * STRIPE, (n + 1) * STRIPE)
        o = wide[part]
        factor = lax.rsqrt(jnp.mean(o * o, axis=1, keepdims=True) + EPSILON)
        y = o * factor
        live = (row_slot[:STRIPE] < lengths[n]).astype(jnp.float32)
        g = qg[n, 1].astype(jnp.float32) * live
        d_out = factor * (g - y * jnp.mean(g * y, axis=1, keepdims=True))
        dos[part] = d_out.astype(jnp.bfloat16)
    d_out = dos[...]

    stat1[...] = jnp.zeros((ROWS, 128), jnp.float32)
    stat2[...] = jnp.zeros((ROWS, 128), jnp.float32)
    for j in range(GROUPS):
        lo = j * TILE

        for step in range(STEPS):
            cols = slice(step * STEP, (step + 1) * STEP)
            da = dot_nt(d_out[lo:], values(j, slice(SPAN * step, SPAN * step + SPAN)))
            das[of(j), cols] = da
            stat1[lo:] += fold(jnp.add, da * p1s[of(j), cols])
            stat2[lo:] += fold(jnp.add, da * p2s[of(j), cols])

    e1 = jnp.sum(stat1[...], axis=1, keepdims=True) * inv1
    e2 = jnp.sum(stat2[...], axis=1, keepdims=True) * inv2

    wide[...] = jnp.zeros((ROWS, WIDTH), jnp.float32)
    out_copies = []

    def send(src, dst):
        copy = pltpu.make_async_copy(src, dst, out_sems.at[len(out_copies)])
        copy.start()
        out_copies.append(copy)

    for j in range(GROUPS):
        lo = j * TILE

        for step in range(STEPS):
            cols = slice(step * STEP, (step + 1) * STEP)
            da = das[of(j), cols]
            t1 = p1s[of(j), cols] * (inv1[lo:] * (da - e1[lo:]))
            t2 = p2s[of(j), cols] * (inv2[lo:] * (da - e2[lo:]))
            t1s[of(j), cols] = t1.astype(jnp.bfloat16)
            t2s[of(j), cols] = t2.astype(jnp.bfloat16)

        k = keys(j)
        wide[lo:, :HALF] += dot_nn(t1s[of(j)], k[:, :HALF])
        wide[lo:, HALF:] += dot_nn(t2s[of(j)], k[:, HALF:])

        for step in range(STEPS):
            cols = slice(step * STEP, (step + 1) * STEP)
            dk1 = dot_tn(q1[lo:], t1s[of(j), cols]) * SCALE
            dk2 = dot_tn(q2[lo:], t2s[of(j), cols]) * (-SCALE * weight)
            dk = jnp.concatenate([dk1, dk2], axis=0)
            dv = dot_tn(d_out[lo:], mixs[of(j), cols])
            parts = slice(SPAN * step, SPAN * step + SPAN)
            for kind, x in ((0, dk), (1, dv)):
                outs[j // HALVES, parts, j % HALVES, :, kind] = (
                    x.T.astype(jnp.bfloat16).reshape(SPAN, NEXT, STRIPE, WIDTH)
                )

        for u in range(PARTS):
            half, at = j // HALVES, j % HALVES
            send(outs.at[half, where[u], at], term_outs[2 * u + half].at[at])

    dq[:, :, :HALF] = (wide[:, :HALF] * SCALE).astype(jnp.bfloat16).reshape(SLICES, STRIPE, HALF)
    dq[:, :, HALF:] = (
        (wide[:, HALF:] * (-SCALE * weight)).astype(jnp.bfloat16).reshape(SLICES, STRIPE, HALF)
    )
    send(dq, dq_out)
    for copy in out_copies:
        copy.wait()


def core(lengths, where, lams, qg, kv_halves):
    smem = pl.BlockSpec(memory_space=pltpu.SMEM)
    hbm = pl.BlockSpec(memory_space=pl.ANY)
    b16, f32 = jnp.bfloat16, jnp.float32
    halves = [x.reshape(HALVES, NEXT, 2, STRIPE, WIDTH) for x in kv_halves]
    d_query, *terms = pl.pallas_call(
        core_kernel,
        out_shape=(
            jax.ShapeDtypeStruct((SLICES, STRIPE, WIDTH), b16),
        )
        + (jax.ShapeDtypeStruct((HALVES, NEXT, 2, STRIPE, WIDTH), b16),) * (2 * PARTS),
        in_specs=[smem, smem, smem, hbm] + [hbm] * (2 * PARTS),
        out_specs=(hbm,) + (hbm,) * (2 * PARTS),
        scratch_shapes=[
            pltpu.VMEM((SLICES, 2, STRIPE, WIDTH), b16),
            pltpu.VMEM((SLICES, STRIPE, WIDTH), b16),
            pltpu.VMEM((GROUPS, PARTS, NEXT, 2, STRIPE, WIDTH), b16),
            pltpu.VMEM((STORED, CHUNK), f32),
            pltpu.VMEM((STORED, CHUNK), f32),
            pltpu.VMEM((STORED, CHUNK), f32),
            pltpu.VMEM((STORED, CHUNK), b16),
            pltpu.VMEM((STORED, CHUNK), b16),
            pltpu.VMEM((STORED, CHUNK), b16),
            pltpu.VMEM((2, PARTS, HALVES, NEXT, 2, STRIPE, WIDTH), b16),
            pltpu.VMEM((ROWS, 128), f32),
            pltpu.VMEM((ROWS, 128), f32),
            pltpu.VMEM((ROWS, WIDTH), f32),
            pltpu.VMEM((ROWS, WIDTH), b16),
            pltpu.SemaphoreType.DMA((1 + PARTS * 4,)),
            pltpu.SemaphoreType.DMA((1 + PARTS * GROUPS,)),
        ],
        compiler_params=pltpu.CompilerParams(vmem_limit_bytes=60 * 1024 * 1024),
        name="attention",
    )(lengths, where, lams, qg, *halves)
    return d_query, *[x.reshape(SLICES // 2, 2, STRIPE, WIDTH) for x in terms]


def final_kernel(*refs):
    d_query, *ins, out = refs
    out[:, 0] = d_query[...]
    for half in range(2):
        total = ins[half][...].astype(jnp.float32)
        for x in ins[2 + half :: 2]:
            total = total + x[...].astype(jnp.float32)
        out[8 * half : 8 * half + 8, 1:] = total.astype(out.dtype)


def final(d_query, *halves):
    return pl.pallas_call(
        final_kernel,
        out_shape=jax.ShapeDtypeStruct((SLICES, 3, STRIPE, WIDTH), jnp.bfloat16),
        in_specs=[pl.BlockSpec(memory_space=pltpu.VMEM)] * (1 + len(halves)),
        out_specs=pl.BlockSpec(memory_space=pltpu.VMEM),
        name="final",
    )(d_query, *halves)


def along_z(x, d):
    return lax.ppermute(x, "z", [(i, (i + d) % 4) for i in range(4)])


def swap(x):
    return lax.ppermute(x, "core", [(0, 1), (1, 0)])


def shards(queries, keys, values, out_grad, lam, lengths):
    z, c = lax.axis_index("z"), lax.axis_index("core")
    section = lax.axis_index("x") * 4 + lax.axis_index("y")
    where = jnp.stack(
        [2 * ((z - d) % 4) + c for d in range(4)]
        + [2 * ((z - d) % 4) + 1 - c for d in range(4)]
        + [section]
    ).astype(jnp.int32)

    kv = lax.all_to_all(pack(keys, values), SECTION, 0, 0, tiled=True)
    lams = lax.ppermute(
        lam, ALL, [(s * 8 + t, (2 * t + s // 8) * 8 + s % 8) for s in range(SLICES) for t in range(PARTS)]
    )
    kv, qg, lams, where = lax.optimization_barrier((kv, pack(queries, out_grad), lams, where))
    lower, upper = lax.optimization_barrier((kv[:8], kv[8:]))
    lower_up, upper_down = along_z(lower, 1), along_z(upper, -1)
    upper_up, lower_down = along_z(upper, 1), along_z(lower, -1)
    lower_far, upper_far = along_z(lower_up, 1), along_z(upper_down, -1)
    qg = lax.all_to_all(qg, SECTION, 0, 0, tiled=True)
    upper_up, lower_down, qg = lax.optimization_barrier((upper_up, lower_down, qg))
    near = [lower, upper, lower_up, upper_up, lower_far, upper_far, lower_down, upper_down]

    d_query, *terms = core(lengths, where, lams, qg, near + [swap(x) for x in near])

    def add(*xs):
        return sum(x.astype(jnp.float32) for x in xs).astype(jnp.bfloat16)

    own, other = terms[:PARTS], [swap(x) for x in terms[PARTS:]]
    lower_far = along_z(add(own[4], other[4]), -1)
    upper_far = along_z(add(own[5], other[5]), 1)
    upper_1 = along_z(add(own[3], other[3]), -1)
    lower_3 = along_z(add(own[6], other[6]), 1)
    lower_1 = along_z(add(own[2], other[2], lower_far), -1)
    upper_3 = along_z(add(own[7], other[7], upper_far), 1)
    total = final(d_query, own[0], own[1], other[0], other[1], lower_3, upper_1, lower_1, upper_3)
    return unpack(lax.all_to_all(total, SECTION, 0, 0, tiled=True))


def solution(mesh):
    fine = Mesh(mesh.devices.reshape(4, 4, 4, 2), ("x", "y", "z", "core"))
    rows = P(ALL, None)
    return jax.shard_map(
        shards,
        mesh=fine,
        in_specs=(rows, rows, rows, rows, P(("z", "core")), P()),
        out_specs=(rows, rows, rows),
        check_vma=False,
    )
```

```python
import functools

import jax
import jax.numpy as jnp
from jax import lax
from jax.experimental import pallas as pl
from jax.experimental.pallas import tpu as pltpu
from jax.sharding import Mesh
from jax.sharding import PartitionSpec as P

EPSILON = 1e-05
NEGATIVE = -1e30
LOG2E = 1.4426950408889634

STRIPE = 32
SLICES = 16
PARTS = 8
WIDTH = 256
HALF = 128
ROWS = SLICES * STRIPE
TILE = 64
NEXT = TILE // STRIPE
GROUPS = ROWS // TILE
CHUNK = PARTS * TILE
STORED = sum(ROWS - j * TILE for j in range(GROUPS))
STEP = 256
SPAN = STEP // TILE
STEPS = PARTS // SPAN
HALVES = GROUPS // 2
LIVE_STEPS = STEPS // 2
SECTION = ("x", "y")
ALL = ("x", "y", "z", "core")
SCALE = HALF ** (-0.5)


def pack_kernel(a_ref, b_ref, out_ref):
    for head in range(SLICES):
        cols = slice(head * WIDTH, (head + 1) * WIDTH)
        out_ref[head, 0] = a_ref[:, cols]
        out_ref[head, 1] = b_ref[:, cols]


def pack(a, b):
    return pl.pallas_call(
        pack_kernel,
        out_shape=jax.ShapeDtypeStruct((SLICES, 2, STRIPE, WIDTH), a.dtype),
        in_specs=[pl.BlockSpec(memory_space=pltpu.VMEM)] * 2,
        out_specs=pl.BlockSpec(memory_space=pltpu.VMEM),
        name="pack",
    )(a, b)


def unpack_kernel(in_ref, *outs):
    for head in range(SLICES):
        for i, out in enumerate(outs):
            out[:, head * WIDTH : (head + 1) * WIDTH] = in_ref[head, i]


def unpack(x):
    shape = jax.ShapeDtypeStruct((STRIPE, SLICES * WIDTH), x.dtype)
    return pl.pallas_call(
        unpack_kernel,
        out_shape=(shape,) * 3,
        in_specs=[pl.BlockSpec(memory_space=pltpu.VMEM)],
        out_specs=(pl.BlockSpec(memory_space=pltpu.VMEM),) * 3,
        name="unpack",
    )(x)


def dot_nt(a, b):
    return lax.dot_general(a, b, (((1,), (1,)), ((), ())), preferred_element_type=jnp.float32)


def dot_nn(a, b):
    return lax.dot_general(a, b, (((1,), (0,)), ((), ())), preferred_element_type=jnp.float32)


def dot_tn(a, b):
    return lax.dot_general(a, b, (((0,), (0,)), ((), ())), preferred_element_type=jnp.float32)


def fold(op, x):
    out = x[:, :128]
    for c in range(1, x.shape[1] // 128):
        out = op(out, x[:, c * 128 : (c + 1) * 128])
    return out


def core_kernel(lengths, where, lams, qg_in, *refs):
    kv_halves = refs[: 2 * PARTS]
    dq_out, *term_outs = refs[2 * PARTS : 4 * PARTS + 1]
    qg, dq, kvs, p1s, p2s, das, mixs, t1s, t2s, outs, stat1, stat2, wide, dos, in_sems, out_sems = refs[
        4 * PARTS + 1 :
    ]

    copies = {}

    def fetch(name, src, dst):
        copy = pltpu.make_async_copy(src, dst, in_sems.at[sum(map(len, copies.values()))])
        copy.start()
        copies.setdefault(name, []).append(copy)

    def arrived(*name):
        for copy in copies[name]:
            copy.wait()

    fetch(("queries",), qg_in, qg)
    for kind in range(2):
        for half in range(2):
            for u in range(PARTS):
                chunks = slice(half * HALVES, (half + 1) * HALVES)
                fetch((kind, half), kv_halves[2 * u + half].at[:, :, kind], kvs.at[chunks, where[u], :, kind])

    def keys(j, parts=slice(0, PARTS)):
        return kvs[j, parts, :, 0].reshape(-1, WIDTH)

    def values(j, parts=slice(0, PARTS)):
        return kvs[j, parts, :, 1].reshape(-1, WIDTH)

    def of(j, skip=0, count=None):
        first = sum(ROWS - i * TILE for i in range(j)) + skip
        return slice(first, first + (ROWS - j * TILE - skip if count is None else count))

    lane = lax.broadcasted_iota(jnp.int32, (1, STEP), 1)
    lane_slice = lane % TILE // STRIPE

    weight = lams[where[PARTS] % 2]
    row = lax.broadcasted_iota(jnp.int32, (ROWS, 1), 0)
    row_slot = where[0] * STRIPE + row % STRIPE
    tile_pos = 256 * (row[:TILE] // STRIPE) + row_slot[:TILE]
    arrived("queries")
    q = qg[:, 0].reshape(ROWS, WIDTH)
    q1, q2 = q[:, :HALF], q[:, HALF:]
    stat1[...] = jnp.full((ROWS, 128), NEGATIVE, jnp.float32)
    stat2[...] = jnp.full((ROWS, 128), NEGATIVE, jnp.float32)

    for j in range(GROUPS):
        lo = j * TILE
        if j % HALVES == 0:
            arrived(0, j // HALVES)

        for step in range(STEPS):
            k = keys(j, slice(SPAN * step, SPAN * step + SPAN))
            cols = slice(step * STEP, (step + 1) * STEP)
            slot = (SPAN * step + lane // TILE) * STRIPE + lane % STRIPE
            vis = 256 * lane_slice + slot <= tile_pos
            if step >= LIVE_STEPS:
                length = jnp.full((1, STEP), lengths[NEXT * j], jnp.int32)
                for nl in range(1, NEXT):
                    length = jnp.where(lane_slice == nl, lengths[NEXT * j + nl], length)
                vis = vis & (slot < length)
                hide = jnp.where(slot < length, 0.0, NEGATIVE)
            for half, p, stat in ((0, p1s, stat1), (HALF, p2s, stat2)):
                scores = dot_nt(q[lo:, half : half + HALF], k[:, half : half + HALF])
                top, rest = jnp.where(vis, scores[:TILE], NEGATIVE), scores[TILE:]
                p[of(j, 0, TILE), cols] = top
                stat[lo : lo + TILE] = jnp.maximum(stat[lo : lo + TILE], fold(jnp.maximum, top))
                if j < GROUPS - 1:
                    rest = rest + hide if step >= LIVE_STEPS else rest
                    p[of(j, TILE), cols] = rest
                    stat[lo + TILE :] = jnp.maximum(stat[lo + TILE :], fold(jnp.maximum, rest))

    m1 = jnp.max(stat1[...], axis=1, keepdims=True)
    m2 = jnp.max(stat2[...], axis=1, keepdims=True)
    stat1[...] = jnp.zeros((ROWS, 128), jnp.float32)
    stat2[...] = jnp.zeros((ROWS, 128), jnp.float32)
    for j in range(GROUPS):
        lo = j * TILE

        for step in range(STEPS):
            cols = slice(step * STEP, (step + 1) * STEP)
            p1 = jnp.exp2((p1s[of(j), cols] - m1[lo:]) * (SCALE * LOG2E))
            p2 = jnp.exp2((p2s[of(j), cols] - m2[lo:]) * (SCALE * LOG2E))
            p1s[of(j), cols] = p1
            p2s[of(j), cols] = p2
            stat1[lo:] += fold(jnp.add, p1)
            stat2[lo:] += fold(jnp.add, p2)

    inv1 = 1.0 / jnp.sum(stat1[...], axis=1, keepdims=True)
    inv2 = 1.0 / jnp.sum(stat2[...], axis=1, keepdims=True)
    winv2 = weight * inv2

    wide[...] = jnp.zeros((ROWS, WIDTH), jnp.float32)
    for j in range(GROUPS):
        lo = j * TILE
        if j % HALVES == 0:
            arrived(1, j // HALVES)

        for step in range(STEPS):
            cols = slice(step * STEP, (step + 1) * STEP)
            a = p1s[of(j), cols] * inv1[lo:] - p2s[of(j), cols] * winv2[lo:]
            mixs[of(j), cols] = a.astype(jnp.bfloat16)

        wide[lo:] += dot_nn(mixs[of(j)], values(j))

    for n in range(SLICES):
        part = slice(n * STRIPE, (n + 1) * STRIPE)
        o = wide[part]
        factor = lax.rsqrt(jnp.mean(o * o, axis=1, keepdims=True) + EPSILON)
        y = o * factor
        live = (row_slot[:STRIPE] < lengths[n]).astype(jnp.float32)
        g = qg[n, 1].astype(jnp.float32) * live
        d_out = factor * (g - y * jnp.mean(g * y, axis=1, keepdims=True))
        dos[part] = d_out.astype(jnp.bfloat16)
    d_out = dos[...]

    stat1[...] = jnp.zeros((ROWS, 128), jnp.float32)
    stat2[...] = jnp.zeros((ROWS, 128), jnp.float32)
    for j in range(GROUPS):
        lo = j * TILE

        for step in range(STEPS):
            cols = slice(step * STEP, (step + 1) * STEP)
            da = dot_nt(d_out[lo:], values(j, slice(SPAN * step, SPAN * step + SPAN)))
            das[of(j), cols] = da
            stat1[lo:] += fold(jnp.add, da * p1s[of(j), cols])
            stat2[lo:] += fold(jnp.add, da * p2s[of(j), cols])

    e1 = jnp.sum(stat1[...], axis=1, keepdims=True) * inv1
    e2 = jnp.sum(stat2[...], axis=1, keepdims=True) * inv2

    wide[...] = jnp.zeros((ROWS, WIDTH), jnp.float32)
    out_copies = []

    def send(src, dst):
        copy = pltpu.make_async_copy(src, dst, out_sems.at[len(out_copies)])
        copy.start()
        out_copies.append(copy)

    for j in range(GROUPS):
        lo = j * TILE

        for step in range(STEPS):
            cols = slice(step * STEP, (step + 1) * STEP)
            da = das[of(j), cols]
            t1 = p1s[of(j), cols] * (inv1[lo:] * (da - e1[lo:]))
            t2 = p2s[of(j), cols] * (inv2[lo:] * (da - e2[lo:]))
            t1s[of(j), cols] = t1.astype(jnp.bfloat16)
            t2s[of(j), cols] = t2.astype(jnp.bfloat16)

        k = keys(j)
        wide[lo:, :HALF] += dot_nn(t1s[of(j)], k[:, :HALF])
        wide[lo:, HALF:] += dot_nn(t2s[of(j)], k[:, HALF:])

        for step in range(STEPS):
            cols = slice(step * STEP, (step + 1) * STEP)
            dk1 = dot_tn(q1[lo:], t1s[of(j), cols]) * SCALE
            dk2 = dot_tn(q2[lo:], t2s[of(j), cols]) * (-SCALE * weight)
            dk = jnp.concatenate([dk1, dk2], axis=0)
            dv = dot_tn(d_out[lo:], mixs[of(j), cols])
            parts = slice(SPAN * step, SPAN * step + SPAN)
            for kind, x in ((0, dk), (1, dv)):
                outs[j // HALVES, parts, j % HALVES, :, kind] = (
                    x.T.astype(jnp.bfloat16).reshape(SPAN, NEXT, STRIPE, WIDTH)
                )

        for u in range(PARTS):
            half, at = j // HALVES, j % HALVES
            send(outs.at[half, where[u], at], term_outs[2 * u + half].at[at])

    dq[:, :, :HALF] = (wide[:, :HALF] * SCALE).astype(jnp.bfloat16).reshape(SLICES, STRIPE, HALF)
    dq[:, :, HALF:] = (
        (wide[:, HALF:] * (-SCALE * weight)).astype(jnp.bfloat16).reshape(SLICES, STRIPE, HALF)
    )
    send(dq, dq_out)
    for copy in out_copies:
        copy.wait()


def core(lengths, where, lams, qg, kv_halves):
    smem = pl.BlockSpec(memory_space=pltpu.SMEM)
    hbm = pl.BlockSpec(memory_space=pl.ANY)
    b16, f32 = jnp.bfloat16, jnp.float32
    halves = [x.reshape(HALVES, NEXT, 2, STRIPE, WIDTH) for x in kv_halves]
    d_query, *terms = pl.pallas_call(
        core_kernel,
        out_shape=(
            jax.ShapeDtypeStruct((SLICES, STRIPE, WIDTH), b16),
        )
        + (jax.ShapeDtypeStruct((HALVES, NEXT, 2, STRIPE, WIDTH), b16),) * (2 * PARTS),
        in_specs=[smem, smem, smem, hbm] + [hbm] * (2 * PARTS),
        out_specs=(hbm,) + (hbm,) * (2 * PARTS),
        scratch_shapes=[
            pltpu.VMEM((SLICES, 2, STRIPE, WIDTH), b16),
            pltpu.VMEM((SLICES, STRIPE, WIDTH), b16),
            pltpu.VMEM((GROUPS, PARTS, NEXT, 2, STRIPE, WIDTH), b16),
            pltpu.VMEM((STORED, CHUNK), f32),
            pltpu.VMEM((STORED, CHUNK), f32),
            pltpu.VMEM((STORED, CHUNK), f32),
            pltpu.VMEM((STORED, CHUNK), b16),
            pltpu.VMEM((STORED, CHUNK), b16),
            pltpu.VMEM((STORED, CHUNK), b16),
            pltpu.VMEM((2, PARTS, HALVES, NEXT, 2, STRIPE, WIDTH), b16),
            pltpu.VMEM((ROWS, 128), f32),
            pltpu.VMEM((ROWS, 128), f32),
            pltpu.VMEM((ROWS, WIDTH), f32),
            pltpu.VMEM((ROWS, WIDTH), b16),
            pltpu.SemaphoreType.DMA((1 + PARTS * 4,)),
            pltpu.SemaphoreType.DMA((1 + PARTS * GROUPS,)),
        ],
        compiler_params=pltpu.CompilerParams(vmem_limit_bytes=60 * 1024 * 1024),
        name="attention",
    )(lengths, where, lams, qg, *halves)
    return d_query, *[x.reshape(SLICES // 2, 2, STRIPE, WIDTH) for x in terms]


def gather_kernel(d_query, *refs):
    *ins, out = refs
    out[:, 0] = d_query[...]
    for half in range(2):
        total = ins[half][...].astype(jnp.float32)
        for x in ins[2 + half :: 2]:
            total = total + x[...].astype(jnp.float32)
        out[8 * half : 8 * half + 8, 1:] = total.astype(out.dtype)


def gradients(kernel, name, *args):
    return pl.pallas_call(
        kernel,
        out_shape=jax.ShapeDtypeStruct((SLICES, 3, STRIPE, WIDTH), jnp.bfloat16),
        in_specs=[pl.BlockSpec(memory_space=pltpu.VMEM)] * len(args),
        out_specs=pl.BlockSpec(memory_space=pltpu.VMEM),
        cost_estimate=pl.CostEstimate(flops=10**6, bytes_accessed=3 * 10**6, transcendentals=0),
        name=name,
    )(*args)


def along_z(x, d):
    return lax.ppermute(x, "z", [(i, (i + d) % 4) for i in range(4)])


def swap(x):
    return lax.ppermute(x, "core", [(0, 1), (1, 0)])


def shards(queries, keys, values, out_grad, lam, lengths):
    z, c = lax.axis_index("z"), lax.axis_index("core")
    section = lax.axis_index("x") * 4 + lax.axis_index("y")
    where = jnp.stack(
        [2 * ((z - d) % 4) + c for d in range(4)]
        + [2 * ((z - d) % 4) + 1 - c for d in range(4)]
        + [section]
    ).astype(jnp.int32)

    kv = lax.all_to_all(pack(keys, values), SECTION, 0, 0, tiled=True)
    lams = lax.ppermute(
        lam, ALL, [(s * 8 + t, (2 * t + s // 8) * 8 + s % 8) for s in range(SLICES) for t in range(PARTS)]
    )
    kv, qg, lams, where = lax.optimization_barrier((kv, pack(queries, out_grad), lams, where))
    lower, upper = lax.optimization_barrier((kv[:8], kv[8:]))
    lower_up, upper_down = along_z(lower, 1), along_z(upper, -1)
    upper_up, lower_down = along_z(upper, 1), along_z(lower, -1)
    lower_far, upper_far = along_z(lower_up, 1), along_z(upper_down, -1)
    qg = lax.all_to_all(qg, SECTION, 0, 0, tiled=True)
    upper_up, lower_down, qg = lax.optimization_barrier((upper_up, lower_down, qg))
    near = [lower, upper, lower_up, upper_up, lower_far, upper_far, lower_down, upper_down]

    d_query, *terms = core(lengths, where, lams, qg, near + [swap(x) for x in near])

    def add(*xs):
        return sum(x.astype(jnp.float32) for x in xs).astype(jnp.bfloat16)

    own, other = terms[:PARTS], [swap(x) for x in terms[PARTS:]]
    lower_far = along_z(add(own[4], other[4]), -1)
    upper_far = along_z(add(own[5], other[5]), 1)
    upper_1 = along_z(add(own[3], other[3]), -1)
    lower_3 = along_z(add(own[6], other[6]), 1)
    lower_1 = along_z(add(own[2], other[2], lower_far), -1)
    upper_3 = along_z(add(own[7], other[7], upper_far), 1)
    gathered = gradients(
        gather_kernel, "gather", d_query, own[0], own[1], other[0], other[1], lower_3, upper_1
    )
    last = jnp.pad(jnp.concatenate([lower_1, upper_3], axis=0), ((0, 0), (1, 0), (0, 0), (0, 0)))
    total = add(gathered, last)
    return unpack(lax.all_to_all(total, SECTION, 0, 0, tiled=True))


def solution(mesh):
    fine = Mesh(mesh.devices.reshape(4, 4, 4, 2), ("x", "y", "z", "core"))
    rows = P(ALL, None)
    return jax.shard_map(
        shards,
        mesh=fine,
        in_specs=(rows, rows, rows, rows, P(("z", "core")), P()),
        out_specs=(rows, rows, rows),
        check_vma=False,
    )
```

```python
import functools

import jax
import jax.numpy as jnp
from jax import lax
from jax.experimental import pallas as pl
from jax.experimental.pallas import tpu as pltpu
from jax.sharding import Mesh
from jax.sharding import PartitionSpec as P

EPSILON = 1e-05
NEGATIVE = -1e30
LOG2E = 1.4426950408889634

STRIPE = 32
SLICES = 16
PARTS = 8
WIDTH = 256
HALF = 128
ROWS = SLICES * STRIPE
TILE = 64
NEXT = TILE // STRIPE
GROUPS = ROWS // TILE
CHUNK = PARTS * TILE
STORED = sum(ROWS - j * TILE for j in range(GROUPS))
STEP = 256
SPAN = STEP // TILE
STEPS = PARTS // SPAN
HALVES = GROUPS // 2
LIVE_STEPS = STEPS // 2
SECTION = ("x", "y")
ALL = ("x", "y", "z", "core")
SCALE = HALF ** (-0.5)


def pack_kernel(a_ref, b_ref, out_ref):
    for head in range(SLICES):
        cols = slice(head * WIDTH, (head + 1) * WIDTH)
        out_ref[head, 0] = a_ref[:, cols]
        out_ref[head, 1] = b_ref[:, cols]


def pack(a, b):
    return pl.pallas_call(
        pack_kernel,
        out_shape=jax.ShapeDtypeStruct((SLICES, 2, STRIPE, WIDTH), a.dtype),
        in_specs=[pl.BlockSpec(memory_space=pltpu.VMEM)] * 2,
        out_specs=pl.BlockSpec(memory_space=pltpu.VMEM),
        name="pack",
    )(a, b)


def unpack_kernel(in_ref, *outs):
    for head in range(SLICES):
        for i, out in enumerate(outs):
            out[:, head * WIDTH : (head + 1) * WIDTH] = in_ref[head, i]


def unpack(x):
    shape = jax.ShapeDtypeStruct((STRIPE, SLICES * WIDTH), x.dtype)
    return pl.pallas_call(
        unpack_kernel,
        out_shape=(shape,) * 3,
        in_specs=[pl.BlockSpec(memory_space=pltpu.VMEM)],
        out_specs=(pl.BlockSpec(memory_space=pltpu.VMEM),) * 3,
        name="unpack",
    )(x)


def dot_nt(a, b):
    return lax.dot_general(a, b, (((1,), (1,)), ((), ())), preferred_element_type=jnp.float32)


def dot_nn(a, b):
    return lax.dot_general(a, b, (((1,), (0,)), ((), ())), preferred_element_type=jnp.float32)


def dot_tn(a, b):
    return lax.dot_general(a, b, (((0,), (0,)), ((), ())), preferred_element_type=jnp.float32)


def fold(op, x):
    out = x[:, :128]
    for c in range(1, x.shape[1] // 128):
        out = op(out, x[:, c * 128 : (c + 1) * 128])
    return out


def core_kernel(lengths, where, lams, qg_in, *refs):
    kv_halves = refs[: 2 * PARTS]
    dq_out, *term_outs = refs[2 * PARTS : 4 * PARTS + 1]
    qg, dq, kvs, p1s, p2s, das, mixs, t1s, t2s, outs, stat1, stat2, wide, dos, in_sems, out_sems = refs[
        4 * PARTS + 1 :
    ]

    copies = {}

    def fetch(name, src, dst):
        copy = pltpu.make_async_copy(src, dst, in_sems.at[sum(map(len, copies.values()))])
        copy.start()
        copies.setdefault(name, []).append(copy)

    def arrived(*name):
        for copy in copies[name]:
            copy.wait()

    fetch(("queries",), qg_in, qg)
    for kind in range(2):
        for half in range(2):
            for u in range(PARTS):
                chunks = slice(half * HALVES, (half + 1) * HALVES)
                fetch((kind, half), kv_halves[2 * u + half].at[:, :, kind], kvs.at[chunks, where[u], :, kind])

    def keys(j, parts=slice(0, PARTS)):
        return kvs[j, parts, :, 0].reshape(-1, WIDTH)

    def values(j, parts=slice(0, PARTS)):
        return kvs[j, parts, :, 1].reshape(-1, WIDTH)

    def of(j, skip=0, count=None):
        first = sum(ROWS - i * TILE for i in range(j)) + skip
        return slice(first, first + (ROWS - j * TILE - skip if count is None else count))

    lane = lax.broadcasted_iota(jnp.int32, (1, STEP), 1)
    lane_slice = lane % TILE // STRIPE

    weight = lams[where[PARTS] % 2]
    row = lax.broadcasted_iota(jnp.int32, (ROWS, 1), 0)
    row_slot = where[0] * STRIPE + row % STRIPE
    tile_pos = 256 * (row[:TILE] // STRIPE) + row_slot[:TILE]
    arrived("queries")
    q = qg[:, 0].reshape(ROWS, WIDTH)
    q1, q2 = q[:, :HALF], q[:, HALF:]
    stat1[...] = jnp.full((ROWS, 128), NEGATIVE, jnp.float32)
    stat2[...] = jnp.full((ROWS, 128), NEGATIVE, jnp.float32)

    for j in range(GROUPS):
        lo = j * TILE
        if j % HALVES == 0:
            arrived(0, j // HALVES)

        for step in range(STEPS):
            k = keys(j, slice(SPAN * step, SPAN * step + SPAN))
            cols = slice(step * STEP, (step + 1) * STEP)
            slot = (SPAN * step + lane // TILE) * STRIPE + lane % STRIPE
            vis = 256 * lane_slice + slot <= tile_pos
            if step >= LIVE_STEPS:
                length = jnp.full((1, STEP), lengths[NEXT * j], jnp.int32)
                for nl in range(1, NEXT):
                    length = jnp.where(lane_slice == nl, lengths[NEXT * j + nl], length)
                vis = vis & (slot < length)
                hide = jnp.where(slot < length, 0.0, NEGATIVE)
            for half, p, stat in ((0, p1s, stat1), (HALF, p2s, stat2)):
                scores = dot_nt(q[lo:, half : half + HALF], k[:, half : half + HALF])
                top, rest = jnp.where(vis, scores[:TILE], NEGATIVE), scores[TILE:]
                p[of(j, 0, TILE), cols] = top
                stat[lo : lo + TILE] = jnp.maximum(stat[lo : lo + TILE], fold(jnp.maximum, top))
                if j < GROUPS - 1:
                    rest = rest + hide if step >= LIVE_STEPS else rest
                    p[of(j, TILE), cols] = rest
                    stat[lo + TILE :] = jnp.maximum(stat[lo + TILE :], fold(jnp.maximum, rest))

    m1 = jnp.max(stat1[...], axis=1, keepdims=True)
    m2 = jnp.max(stat2[...], axis=1, keepdims=True)
    stat1[...] = jnp.zeros((ROWS, 128), jnp.float32)
    stat2[...] = jnp.zeros((ROWS, 128), jnp.float32)
    for j in range(GROUPS):
        lo = j * TILE

        for step in range(STEPS):
            cols = slice(step * STEP, (step + 1) * STEP)
            p1 = jnp.exp2((p1s[of(j), cols] - m1[lo:]) * (SCALE * LOG2E))
            p2 = jnp.exp2((p2s[of(j), cols] - m2[lo:]) * (SCALE * LOG2E))
            p1s[of(j), cols] = p1
            p2s[of(j), cols] = p2
            stat1[lo:] += fold(jnp.add, p1)
            stat2[lo:] += fold(jnp.add, p2)

    inv1 = 1.0 / jnp.sum(stat1[...], axis=1, keepdims=True)
    inv2 = 1.0 / jnp.sum(stat2[...], axis=1, keepdims=True)
    winv2 = weight * inv2

    wide[...] = jnp.zeros((ROWS, WIDTH), jnp.float32)
    for j in range(GROUPS):
        lo = j * TILE
        if j % HALVES == 0:
            arrived(1, j // HALVES)

        for step in range(STEPS):
            cols = slice(step * STEP, (step + 1) * STEP)
            a = p1s[of(j), cols] * inv1[lo:] - p2s[of(j), cols] * winv2[lo:]
            mixs[of(j), cols] = a.astype(jnp.bfloat16)

        wide[lo:] += dot_nn(mixs[of(j)], values(j))

    for n in range(SLICES):
        part = slice(n * STRIPE, (n + 1) * STRIPE)
        o = wide[part]
        factor = lax.rsqrt(jnp.mean(o * o, axis=1, keepdims=True) + EPSILON)
        y = o * factor
        live = (row_slot[:STRIPE] < lengths[n]).astype(jnp.float32)
        g = qg[n, 1].astype(jnp.float32) * live
        d_out = factor * (g - y * jnp.mean(g * y, axis=1, keepdims=True))
        dos[part] = d_out.astype(jnp.bfloat16)
    d_out = dos[...]

    stat1[...] = jnp.zeros((ROWS, 128), jnp.float32)
    stat2[...] = jnp.zeros((ROWS, 128), jnp.float32)
    for j in range(GROUPS):
        lo = j * TILE

        for step in range(STEPS):
            cols = slice(step * STEP, (step + 1) * STEP)
            da = dot_nt(d_out[lo:], values(j, slice(SPAN * step, SPAN * step + SPAN)))
            das[of(j), cols] = da
            stat1[lo:] += fold(jnp.add, da * p1s[of(j), cols])
            stat2[lo:] += fold(jnp.add, da * p2s[of(j), cols])

    e1 = jnp.sum(stat1[...], axis=1, keepdims=True) * inv1
    e2 = jnp.sum(stat2[...], axis=1, keepdims=True) * inv2

    wide[...] = jnp.zeros((ROWS, WIDTH), jnp.float32)
    out_copies = []
    r1 = (q1.astype(jnp.float32) * inv1).astype(jnp.bfloat16)
    r2 = (q2.astype(jnp.float32) * inv2).astype(jnp.bfloat16)

    def send(src, dst):
        copy = pltpu.make_async_copy(src, dst, out_sems.at[len(out_copies)])
        copy.start()
        out_copies.append(copy)

    for j in range(GROUPS):
        lo = j * TILE

        for step in range(STEPS):
            cols = slice(step * STEP, (step + 1) * STEP)
            da = das[of(j), cols]
            t1 = p1s[of(j), cols] * (da - e1[lo:])
            t2 = p2s[of(j), cols] * (da - e2[lo:])
            t1s[of(j), cols] = t1.astype(jnp.bfloat16)
            t2s[of(j), cols] = t2.astype(jnp.bfloat16)

        k = keys(j)
        wide[lo:, :HALF] += dot_nn(t1s[of(j)], k[:, :HALF])
        wide[lo:, HALF:] += dot_nn(t2s[of(j)], k[:, HALF:])

        for step in range(STEPS):
            cols = slice(step * STEP, (step + 1) * STEP)
            dk1 = dot_tn(r1[lo:], t1s[of(j), cols]) * SCALE
            dk2 = dot_tn(r2[lo:], t2s[of(j), cols]) * (-SCALE * weight)
            dk = jnp.concatenate([dk1, dk2], axis=0)
            dv = dot_tn(d_out[lo:], mixs[of(j), cols])
            parts = slice(SPAN * step, SPAN * step + SPAN)
            for kind, x in ((0, dk), (1, dv)):
                outs[j // HALVES, parts, j % HALVES, :, kind] = (
                    x.T.astype(jnp.bfloat16).reshape(SPAN, NEXT, STRIPE, WIDTH)
                )

        for u in range(PARTS):
            half, at = j // HALVES, j % HALVES
            send(outs.at[half, where[u], at], term_outs[2 * u + half].at[at])

    dq[:, :, :HALF] = (wide[:, :HALF] * (inv1 * SCALE)).astype(jnp.bfloat16).reshape(SLICES, STRIPE, HALF)
    dq[:, :, HALF:] = (
        (wide[:, HALF:] * (inv2 * (-SCALE * weight))).astype(jnp.bfloat16).reshape(SLICES, STRIPE, HALF)
    )
    send(dq, dq_out)
    for copy in out_copies:
        copy.wait()


def core(lengths, where, lams, qg, kv_halves):
    smem = pl.BlockSpec(memory_space=pltpu.SMEM)
    hbm = pl.BlockSpec(memory_space=pl.ANY)
    b16, f32 = jnp.bfloat16, jnp.float32
    halves = [x.reshape(HALVES, NEXT, 2, STRIPE, WIDTH) for x in kv_halves]
    d_query, *terms = pl.pallas_call(
        core_kernel,
        out_shape=(
            jax.ShapeDtypeStruct((SLICES, STRIPE, WIDTH), b16),
        )
        + (jax.ShapeDtypeStruct((HALVES, NEXT, 2, STRIPE, WIDTH), b16),) * (2 * PARTS),
        in_specs=[smem, smem, smem, hbm] + [hbm] * (2 * PARTS),
        out_specs=(hbm,) + (hbm,) * (2 * PARTS),
        scratch_shapes=[
            pltpu.VMEM((SLICES, 2, STRIPE, WIDTH), b16),
            pltpu.VMEM((SLICES, STRIPE, WIDTH), b16),
            pltpu.VMEM((GROUPS, PARTS, NEXT, 2, STRIPE, WIDTH), b16),
            pltpu.VMEM((STORED, CHUNK), f32),
            pltpu.VMEM((STORED, CHUNK), f32),
            pltpu.VMEM((STORED, CHUNK), f32),
            pltpu.VMEM((STORED, CHUNK), b16),
            pltpu.VMEM((STORED, CHUNK), b16),
            pltpu.VMEM((STORED, CHUNK), b16),
            pltpu.VMEM((2, PARTS, HALVES, NEXT, 2, STRIPE, WIDTH), b16),
            pltpu.VMEM((ROWS, 128), f32),
            pltpu.VMEM((ROWS, 128), f32),
            pltpu.VMEM((ROWS, WIDTH), f32),
            pltpu.VMEM((ROWS, WIDTH), b16),
            pltpu.SemaphoreType.DMA((1 + PARTS * 4,)),
            pltpu.SemaphoreType.DMA((1 + PARTS * GROUPS,)),
        ],
        compiler_params=pltpu.CompilerParams(vmem_limit_bytes=60 * 1024 * 1024),
        name="attention",
    )(lengths, where, lams, qg, *halves)
    return d_query, *[x.reshape(SLICES // 2, 2, STRIPE, WIDTH) for x in terms]


def gather_kernel(d_query, *refs):
    *ins, out = refs
    out[:, 0] = d_query[...]
    for half in range(2):
        total = ins[half][...].astype(jnp.float32)
        for x in ins[2 + half :: 2]:
            total = total + x[...].astype(jnp.float32)
        out[8 * half : 8 * half + 8, 1:] = total.astype(out.dtype)


def gradients(kernel, name, *args):
    return pl.pallas_call(
        kernel,
        out_shape=jax.ShapeDtypeStruct((SLICES, 3, STRIPE, WIDTH), jnp.bfloat16),
        in_specs=[pl.BlockSpec(memory_space=pltpu.VMEM)] * len(args),
        out_specs=pl.BlockSpec(memory_space=pltpu.VMEM),
        cost_estimate=pl.CostEstimate(flops=10**6, bytes_accessed=3 * 10**6, transcendentals=0),
        name=name,
    )(*args)


def along_z(x, d):
    return lax.ppermute(x, "z", [(i, (i + d) % 4) for i in range(4)])


def swap(x):
    return lax.ppermute(x, "core", [(0, 1), (1, 0)])


def shards(queries, keys, values, out_grad, lam, lengths):
    z, c = lax.axis_index("z"), lax.axis_index("core")
    section = lax.axis_index("x") * 4 + lax.axis_index("y")
    where = jnp.stack(
        [2 * ((z - d) % 4) + c for d in range(4)]
        + [2 * ((z - d) % 4) + 1 - c for d in range(4)]
        + [section]
    ).astype(jnp.int32)

    kv = lax.all_to_all(pack(keys, values), SECTION, 0, 0, tiled=True)
    lams = lax.ppermute(
        lam, ALL, [(s * 8 + t, (2 * t + s // 8) * 8 + s % 8) for s in range(SLICES) for t in range(PARTS)]
    )
    kv, qg, lams, where = lax.optimization_barrier((kv, pack(queries, out_grad), lams, where))
    lower, upper = lax.optimization_barrier((kv[:8], kv[8:]))
    lower_up, upper_down = along_z(lower, 1), along_z(upper, -1)
    upper_up, lower_down = along_z(upper, 1), along_z(lower, -1)
    lower_far, upper_far = along_z(lower_up, 1), along_z(upper_down, -1)
    qg = lax.all_to_all(qg, SECTION, 0, 0, tiled=True)
    upper_up, lower_down, qg = lax.optimization_barrier((upper_up, lower_down, qg))
    near = [lower, upper, lower_up, upper_up, lower_far, upper_far, lower_down, upper_down]

    d_query, *terms = core(lengths, where, lams, qg, near + [swap(x) for x in near])

    def add(*xs):
        return sum(x.astype(jnp.float32) for x in xs).astype(jnp.bfloat16)

    own, other = terms[:PARTS], [swap(x) for x in terms[PARTS:]]
    lower_far = along_z(add(own[4], other[4]), -1)
    upper_far = along_z(add(own[5], other[5]), 1)
    upper_1 = along_z(add(own[3], other[3]), -1)
    lower_3 = along_z(add(own[6], other[6]), 1)
    lower_1 = along_z(add(own[2], other[2], lower_far), -1)
    upper_3 = along_z(add(own[7], other[7], upper_far), 1)
    gathered = gradients(
        gather_kernel, "gather", d_query, own[0], own[1], other[0], other[1], lower_3, upper_1
    )
    last = jnp.pad(jnp.concatenate([lower_1, upper_3], axis=0), ((0, 0), (1, 0), (0, 0), (0, 0)))
    total = add(gathered, last)
    return unpack(lax.all_to_all(total, SECTION, 0, 0, tiled=True))


def solution(mesh):
    fine = Mesh(mesh.devices.reshape(4, 4, 4, 2), ("x", "y", "z", "core"))
    rows = P(ALL, None)
    return jax.shard_map(
        shards,
        mesh=fine,
        in_specs=(rows, rows, rows, rows, P(("z", "core")), P()),
        out_specs=(rows, rows, rows),
        check_vma=False,
    )
```
